128 devices in a mesh: dp: 16 (over x, y), pipe: 8 (over z, core).
Axes of the slice: x: 4, y: 4, z: 4, core: 2. Of those that a mesh axis runs over, the one named last changes fastest.
Arguments:
- layer_input: bfloat16 [8, 8192, 8192], P('pipe', 'dp')
- value_grad: bfloat16 [8, 8192, 1024], P('pipe', 'dp')
- master_weight: float32 [8, 8192, 1024], P('pipe', 'dp'), may hold values from -0.75 to 0.75
- moment_one: float32 [8, 8192, 1024], P('pipe', 'dp'), may hold values from -1.5 to 1.5
- moment_two: float32 [8, 8192, 1024], P('pipe', 'dp'), may hold values from 0.001 to 0.05
- overflow_flags: int32 [8, 16], P('pipe', 'dp'), may hold values from 0 to 1, as said below
Outputs:
- new_weight: float32 [8, 8192, 1024], P('pipe', 'dp')
- new_moment_one: float32 [8, 8192, 1024], P('pipe', 'dp')
- new_moment_two: float32 [8, 8192, 1024], P('pipe', 'dp')
The draws below stay inside these ranges and needn't reach their ends.
Inputs may be any that keep to these rules, and one draw needn't show every extreme that they name: `overflow_flags`: 1 marks an overflow; in every draw between one and 4 sections hold a mark, each of them on one or more ranks.
All inputs are finite; a program needn't handle non-finite values.
Results may differ from the reference program's by a relative error of at most 0.0003.
Values may be sent and summed in bfloat16 or wider, within the bound.
No kernel may reach another device: no remote copies, remote signals or barrier semaphores. Data moves between devices by JAX's collectives and lax.ppermute only.
A program may use at most 128 MiB of HBM per device.

```python
import math
import jax
import jax.numpy as jnp
from jax import lax

D = 8192
KV = 1024
SECTIONS = 8
DP_RANKS = 16
TOKENS = 8192


def token_signs(key):
    key = jax.random.fold_in(key, 7)
    bits = jax.random.randint(key, (SECTIONS, TOKENS, 1), 0, 2)
    return (2 * bits - 1).astype(jnp.float32)


def draw_layer_input(key, part):
    signs = token_signs(key)
    key = jax.random.fold_in(key, 1)
    key_base = jax.random.fold_in(key, 0)
    key_scale = jax.random.fold_in(key, 1)
    key_direction = jax.random.fold_in(key, 3)
    base = jax.random.normal(key_base, (SECTIONS, TOKENS, D), jnp.float32)
    direction = jax.random.normal(key_direction, (SECTIONS, 1, D), jnp.float32)
    coherent = 0.5 * signs * direction
    rising = 3.0 ** (jnp.arange(D, dtype=jnp.float32) / (D - 1))
    spread = jnp.exp(jax.random.uniform(key_scale, (D,), jnp.float32) * math.log(10.0))
    values = (base + coherent) * (rising * spread)
    return values.astype(jnp.bfloat16)


def draw_value_grad(key, part):
    signs = token_signs(key)
    key = jax.random.fold_in(key, 2)
    key_base = jax.random.fold_in(key, 0)
    key_scale = jax.random.fold_in(key, 1)
    key_direction = jax.random.fold_in(key, 3)
    base = jax.random.normal(key_base, (SECTIONS, TOKENS, KV), jnp.float32)
    direction = jax.random.normal(key_direction, (SECTIONS, 1, KV), jnp.float32)
    section_fall = (3.0 ** ((SECTIONS - 1 - jnp.arange(SECTIONS, dtype=jnp.float32)) / (SECTIONS - 1))).reshape(SECTIONS, 1, 1)
    spread = jnp.exp(jax.random.uniform(key_scale, (SECTIONS, 1, KV), jnp.float32) * math.log(10.0))
    coherent = 3.0 / math.sqrt(TOKENS) * signs * direction
    values = (base + coherent) / math.sqrt(TOKENS) * spread * section_fall
    return values.astype(jnp.bfloat16)


def draw_overflow_flags(key, part):
    key = jax.random.fold_in(key, 3)
    key_count, key_order, key_bits, key_forced = jax.random.split(key, 4)
    marked = jax.random.randint(key_count, (), 1, SECTIONS // 2 + 1)
    order = jax.random.permutation(key_order, SECTIONS)
    section_mark = (order < marked).astype(jnp.int32)
    bits = jax.random.randint(key_bits, (SECTIONS, DP_RANKS), 0, 2)
    forced = jax.random.randint(key_forced, (SECTIONS, 1), 0, DP_RANKS)
    ranks = jnp.arange(DP_RANKS, dtype=jnp.int32)[None, :]
    chosen = jnp.maximum(bits, (ranks == forced).astype(jnp.int32))
    return (section_mark[:, None] * chosen).astype(jnp.int32)


def level_of(rng, extent, cuts, low, largest):
    def one(dim, shards_of):
        heights = jax.random.uniform(jax.random.fold_in(jax.random.fold_in(rng, 6), dim), (shards_of,), jnp.float32, low / len(cuts), largest / len(cuts))
        return jnp.repeat(jnp.exp(heights), extent[dim] // shards_of).reshape((-1,) + (1,) * (len(extent) - dim - 1))

    level = one(*cuts[0])
    for cut in cuts[1:]:
        level = level * one(*cut)
    return level


def gaussian(own_key, dims, deviation, most, cuts=(), kind=jnp.bfloat16):
    level = level_of(own_key, dims, cuts, -0.22, 0.18) if cuts else 1.0
    result = jax.random.normal(own_key, dims, jnp.float32) * deviation * level
    return jnp.minimum(jnp.maximum(result, -most), most).astype(kind)


def setup_inputs(seed: int = 0) -> dict:
    splits = jax.random.split(jax.random.key(seed), 7)
    layer_input = draw_layer_input(jax.random.fold_in(splits[6], 71), 0)
    value_grad = draw_value_grad(jax.random.fold_in(splits[6], 71), 0)
    master_weight = gaussian(splits[2], (SECTIONS, D, KV), 0.05, 0.75, ((0, 8), (1, 16)), jnp.float32)
    moment_one = gaussian(splits[3], (SECTIONS, D, KV), 0.1, 1.5, ((0, 8), (1, 16)), jnp.float32)
    moment_two = jnp.clip(jnp.exp(math.log(0.05) - 3.912023 * jax.random.uniform(splits[4], (SECTIONS, D, KV), jnp.float32) ** level_of(splits[4], (SECTIONS, D, KV), ((0, 8), (1, 16)), -0.2, 0.2)), 0.001, 0.05)
    overflow_flags = draw_overflow_flags(jax.random.fold_in(splits[6], 71), 0)
    return dict(layer_input=layer_input, value_grad=value_grad, master_weight=master_weight, moment_one=moment_one, moment_two=moment_two, overflow_flags=overflow_flags)


def section_gradient(pair):
    inputs_section, grads_section = pair
    return lax.dot_general(inputs_section, grads_section, (((0,), (0,)), ((), ())), preferred_element_type=jnp.float32)

def reference(layer_input, value_grad, master_weight, moment_one, moment_two, overflow_flags):
    gradient = lax.map(section_gradient, (layer_input, value_grad))
    flagged = lax.optimization_barrier(jnp.max(overflow_flags, axis=1)) != 0
    squares = lax.optimization_barrier(jnp.sum(gradient * gradient, axis=(1, 2)))
    total = jnp.sum(jnp.where(flagged, jnp.float32(0.0), squares))
    bound = 0.5 * math.sqrt(D * KV * SECTIONS)
    clip = jnp.minimum(jnp.float32(1.0), bound / (jnp.sqrt(total) + 1e-06))
    keep = jnp.logical_not(flagged)[:, None, None]
    step = clip * gradient
    first = 0.9 * moment_one + 0.1 * step
    second = 0.95 * moment_two + 0.05 * step * step
    updated = master_weight - 0.02 * (first / (jnp.sqrt(second) + 1e-08) + 0.1 * master_weight)
    new_weight = jnp.where(keep, updated, master_weight)
    new_moment_one = jnp.where(keep, first, moment_one)
    new_moment_two = jnp.where(keep, second, moment_two)
    return (new_weight, new_moment_one, new_moment_two)
```

```python
import functools
import math

import jax
import jax.numpy as jnp
from jax import lax
from jax.experimental import pallas as pl
from jax.experimental.pallas import tpu as pltpu
from jax.sharding import PartitionSpec as P

D = 8192
KV = 1024
RANKS = 16
PIPE = 8
TOK = 512
OWN = 512
COLS = 256
VARIANTS = 4
CHUNKS = 2
ROWS = OWN // CHUNKS
STEP = 64
TOP = 32760.0
SCALE_ROWS = 16

XA, XB, YA, YB = 4, 12, 1, 3
ORDERS = ((XA, XB, YA, YB), (XB, XA, YB, YA), (YA, YB, XA, XB), (YB, YA, XB, XA))


def masks_of(order, step):
    if step == 4:
        return [0]
    out = []
    later = order[step + 1 :]
    for pick in range(1 << len(later)):
        mask = order[step]
        for position, bit in enumerate(later):
            if pick >> (len(later) - 1 - position) & 1:
                mask ^= bit
        out.append(mask)
    return out


def decode(codes, scale):
    wide = codes.astype(jnp.float32)
    return wide * jnp.abs(wide) * scale


def scale_of(step_code):
    power = step_code * (1.0 / 64.0)
    return jnp.exp2(power), jnp.exp2(-power)


def fetch(me_ref, x_ref, x_buf, sems, masks, chunk):
    copies = []
    for slot, mask in enumerate(masks):
        block = jnp.bitwise_xor(me_ref[0], mask)
        start = pl.multiple_of(block * OWN + chunk * ROWS, ROWS)
        copy = pltpu.make_async_copy(
            x_ref.at[0, :, pl.ds(start, ROWS)], x_buf.at[slot], sems.at[slot]
        )
        copy.start()
        copies.append(copy)
    return copies


def sum_blocks(copies, x_buf, g_ref, cols, received, sums, step):
    count = len(copies)
    scales = [
        scale_of(r[r.shape[0] - SCALE_ROWS :, :].astype(jnp.float32)[:1])[0]
        * (1.0 / (TOP * TOP))
        for r in received
    ]
    largest = jnp.zeros((1, COLS), jnp.float32)
    for slot in range(count):
        copies[slot].wait()
        total = lax.dot_general(
            x_buf[slot],
            g_ref[0, :, cols],
            (((0,), (0,)), ((), ())),
            preferred_element_type=jnp.float32,
        )
        for earlier, (r, scale) in enumerate(zip(received, scales)):
            row = (slot + (count if step < 4 else 0)) * ROWS
            total = total + decode(r[row : row + ROWS, :], scale)
        sums[slot * ROWS : (slot + 1) * ROWS, :] = total
        largest = jnp.maximum(largest, jnp.max(jnp.abs(total), axis=0, keepdims=True))
    return largest


def encode(largest, sums, out_ref, rows):
    step_code = jnp.ceil(jnp.log2(jnp.maximum(largest, 1e-37)) * 64.0)
    step_code = jnp.clip(step_code, -90.0 * 64.0, 120.0 * 64.0)
    factor = scale_of(step_code)[1] * (TOP * TOP)
    out_ref[rows : rows + SCALE_ROWS, :] = (
        jnp.broadcast_to(step_code, (SCALE_ROWS, COLS)).astype(jnp.int32).astype(jnp.int16)
    )

    def some(i, _):
        at = pl.ds(pl.multiple_of(i * STEP, STEP), STEP)
        scaled = sums[at, :] * factor
        rooted = scaled * lax.rsqrt(jnp.maximum(jnp.abs(scaled), 1e-12))
        rooted = jnp.clip(jnp.round(rooted), -32767.0, 32767.0)
        out_ref[at, :] = rooted.astype(jnp.int32).astype(jnp.int16)
        return 0

    lax.fori_loop(0, rows // STEP, some, 0)


def send_kernel(step, chunk, variants, *refs):
    me_ref, x_ref, g_ref = refs[:3]
    received = refs[3 : 3 + step * len(variants)]
    outs = refs[3 + step * len(variants) :][: len(variants)]
    x_buf, sums, sems = refs[-3:]
    count = 8 >> step
    copies = [
        fetch(me_ref, x_ref, x_buf.at[i], sems.at[i], masks_of(ORDERS[v], step), chunk)
        for i, v in enumerate(variants)
    ]
    for i, v in enumerate(variants):
        cols = slice(v * COLS, (v + 1) * COLS)
        mine = received[i * step : (i + 1) * step]
        largest = sum_blocks(copies[i], x_buf.at[i], g_ref, cols, mine, sums.at[i], step)
        encode(largest, sums.at[i], outs[i], count * ROWS)


def send(step, chunk, variants, me, layer_input, value_grad, received):
    count = 8 >> step
    n = len(variants)
    whole = pl.BlockSpec(memory_space=pltpu.VMEM)
    flops = 2 * TOK * ROWS * COLS * count * n
    shape = jax.ShapeDtypeStruct((count * ROWS + SCALE_ROWS, COLS), jnp.int16)
    return pl.pallas_call(
        functools.partial(send_kernel, step, chunk, variants),
        out_shape=[shape] * n,
        in_specs=[pl.BlockSpec(memory_space=pltpu.SMEM), pl.BlockSpec(memory_space=pl.ANY)]
        + [whole] * (1 + step * n),
        out_specs=[whole] * n,
        scratch_shapes=[
            pltpu.VMEM((n, count, TOK, ROWS), jnp.bfloat16),
            pltpu.VMEM((n, count * ROWS, COLS), jnp.float32),
            pltpu.SemaphoreType.DMA((n, count)),
        ],
        compiler_params=pltpu.CompilerParams(vmem_limit_bytes=24 << 20),
        cost_estimate=pl.CostEstimate(
            flops=flops,
            bytes_accessed=n * count * (TOK * ROWS * 2 + ROWS * COLS * 2 * (1 + step)),
            transcendentals=n * count * ROWS * COLS,
        ),
        name=f"send_{step}_{chunk}_{variants[0]}",
    )(me, layer_input, value_grad, *[r for v in received for r in v])


def finish_kernel(chunk, *refs):
    me_ref, x_ref, g_ref = refs[:3]
    received = refs[3 : 3 + 4 * VARIANTS]
    grad_ref, squares_ref = refs[3 + 4 * VARIANTS : 5 + 4 * VARIANTS]
    x_buf, sems = refs[-2:]
    [copy] = fetch(me_ref, x_ref, x_buf, sems, [0], chunk)
    copy.wait()
    acc = jnp.zeros((8, 128), jnp.float32)
    for v in range(VARIANTS):
        cols = slice(v * COLS, (v + 1) * COLS)
        total = lax.dot_general(
            x_buf[0],
            g_ref[0, :, cols],
            (((0,), (0,)), ((), ())),
            preferred_element_type=jnp.float32,
        )
        for r in received[4 * v : 4 * v + 4]:
            scale = scale_of(r[r.shape[0] - SCALE_ROWS :, :].astype(jnp.float32)[:1])[0]
            total = total + decode(r[0:ROWS, :], scale * (1.0 / (TOP * TOP)))
        grad_ref[:, cols] = total
        squared = total * total
        for half in range(COLS // 128):
            part = squared[:, half * 128 : (half + 1) * 128]
            acc = acc + jnp.sum(part.reshape(ROWS // 8, 8, 128), axis=0)
    squares_ref[...] = acc


def finish(chunk, me, layer_input, value_grad, received):
    whole = pl.BlockSpec(memory_space=pltpu.VMEM)
    return pl.pallas_call(
        functools.partial(finish_kernel, chunk),
        out_shape=[
            jax.ShapeDtypeStruct((ROWS, KV), jnp.float32),
            jax.ShapeDtypeStruct((8, 128), jnp.float32),
        ],
        in_specs=[pl.BlockSpec(memory_space=pltpu.SMEM), pl.BlockSpec(memory_space=pl.ANY)]
        + [whole] * (1 + 4 * VARIANTS),
        out_specs=[whole] * 2,
        scratch_shapes=[
            pltpu.VMEM((1, TOK, ROWS), jnp.bfloat16),
            pltpu.SemaphoreType.DMA((1,)),
        ],
        compiler_params=pltpu.CompilerParams(vmem_limit_bytes=24 << 20),
        cost_estimate=pl.CostEstimate(
            flops=2 * TOK * ROWS * KV, bytes_accessed=ROWS * KV * 8, transcendentals=0
        ),
        name=f"finish_{chunk}",
    )(me, layer_input, value_grad, *[r for v in received for r in v])


UPDATE_ROWS = 128


def update_kernel(bound, *refs):
    totals, flags_ref, w_ref, m1_ref, m2_ref = refs[:5]
    grads = refs[5 : 5 + CHUNKS]
    new_w, new_m1, new_m2 = refs[5 + CHUNKS :]
    total = jnp.sum(totals[...], keepdims=True)
    clip = jnp.minimum(1.0, bound / (jnp.sqrt(total) + 1e-06))
    keep = jnp.sum(flags_ref[...], keepdims=True) == 0.0
    i = pl.program_id(0)
    w, first_old, second_old = w_ref[0], m1_ref[0], m2_ref[0]

    def body(grad):
        scaled = clip * grad
        first = 0.9 * first_old + 0.1 * scaled
        second = 0.95 * second_old + 0.05 * scaled * scaled
        updated = w - 0.02 * (first / (jnp.sqrt(second) + 1e-08) + 0.1 * w)
        new_w[0] = jnp.where(keep, updated, w)
        new_m1[0] = jnp.where(keep, first, first_old)
        new_m2[0] = jnp.where(keep, second, second_old)

    per = ROWS // UPDATE_ROWS
    for chunk in range(CHUNKS):

        @pl.when(i // per == chunk)
        def _():
            body(grads[chunk][...])


def update(totals, flags, w, m1, m2, grads, bound):
    per = ROWS // UPDATE_ROWS
    block = pl.BlockSpec((1, UPDATE_ROWS, KV), lambda i: (0, i, 0))
    small = pl.BlockSpec((8, 128), lambda i: (0, 0))

    def grad_spec(chunk):
        return pl.BlockSpec(
            (UPDATE_ROWS, KV), lambda i: (jnp.clip(i - chunk * per, 0, per - 1), 0)
        )

    shape = jax.ShapeDtypeStruct((1, OWN, KV), jnp.float32)
    return pl.pallas_call(
        functools.partial(update_kernel, bound),
        grid=(OWN // UPDATE_ROWS,),
        out_shape=[shape] * 3,
        in_specs=[small, small, block, block, block] + [grad_spec(c) for c in range(CHUNKS)],
        out_specs=[block] * 3,
        compiler_params=pltpu.CompilerParams(vmem_limit_bytes=24 << 20),
        name="update",
    )(totals, flags, w, m1, m2, *grads)


def swap(value, axis, count, mask):
    return lax.ppermute(value, axis, [(i, i ^ mask) for i in range(count)])


def spread(value, axis, count, masks):
    arrived = [swap(value, axis, count, mask) for mask in masks]
    return functools.reduce(jnp.add, arrived, value)


def per_device(layer_input, value_grad, master_weight, moment_one, moment_two, overflow_flags):
    me = lax.axis_index("dp").astype(jnp.int32).reshape(1)
    received = [[[] for _ in range(VARIANTS)] for _ in range(CHUNKS)]
    grads, squares = [None] * CHUNKS, [None] * CHUNKS
    for step in range(4):
        for chunk in range(CHUNKS):
            groups = [(v,) for v in range(VARIANTS)] if step < 2 else [tuple(range(VARIANTS))]
            for group in groups:
                codes = send(
                    step, chunk, group, me, layer_input, value_grad,
                    [received[chunk][v] for v in group],
                )
                for v, code in zip(group, codes):
                    received[chunk][v].append(swap(code, "dp", RANKS, ORDERS[v][step]))
    for chunk in range(CHUNKS):
        grads[chunk], squares[chunk] = finish(
            chunk, me, layer_input, value_grad, received[chunk]
        )
    marked = (overflow_flags[0, 0] != 0).astype(jnp.float32)
    own = jnp.concatenate(
        [functools.reduce(jnp.add, squares), jnp.full((8, 128), marked)], axis=0
    )
    section = spread(own, "dp", RANKS, (YA, 2, YB))
    section = spread(section, "dp", RANKS, (XA, 8, XB))
    flags = section[8:]
    masked = jnp.where(flags == 0.0, section[:8], 0.0)
    totals = spread(masked, "pipe", PIPE, (2, 4, 6))
    totals = spread(totals, "pipe", PIPE, (1,))
    bound = 0.5 * math.sqrt(D * KV * PIPE)
    return tuple(
        update(totals, flags, master_weight, moment_one, moment_two, grads, bound)
    )


def solution(mesh):
    placed = P("pipe", "dp", None)
    return jax.shard_map(
        per_device,
        mesh=mesh,
        in_specs=(placed,) * 5 + (P("pipe", "dp"),),
        out_specs=(placed,) * 3,
        check_vma=False,
    )
```

```python
import functools
import math

import jax
import jax.numpy as jnp
from jax import lax
from jax.experimental import pallas as pl
from jax.experimental.pallas import tpu as pltpu
from jax.sharding import PartitionSpec as P

D = 8192
KV = 1024
RANKS = 16
DEVICES = 128
PIPE = 8
TOK = 512
OWN = 512
COLS = 256
VARIANTS = 4
STEP = 128
KERNEL_VMEM = 14 << 20
UPDATE_VMEM = 60 << 20
TOP_POWER = 29.9985
SCALE_ROWS = 16

XA, XB, YA, YB = 4, 12, 1, 3
ORDERS = ((YA, YB, XB, XA), (YB, YA, XA, XB), (XA, XB, YB, YA), (XB, XA, YA, YB))
PAIRS = ((2, 3), (0, 1))


TRANSPOSED = (((0,), (0,)), ((), ()))


def masks_of(order, step):
    base = {0: order[0] ^ order[1], 1: order[0], 2: order[1], 3: 0}[step]
    return [base, base ^ order[3], base ^ order[2], base ^ order[2] ^ order[3]]


def decode(codes, scale):
    wide = codes.astype(jnp.float32)
    return wide * jnp.abs(wide) * scale


def scale_of(step_code):
    power = step_code * (1.0 / 64.0) - TOP_POWER
    return jnp.exp2(power), jnp.exp2(-power)


def columns_of(me_ref, mask):
    block = jnp.bitwise_xor(me_ref[0], mask)
    return pl.ds(pl.multiple_of(block * OWN, OWN), OWN)


def scales_of(received):
    return [
        scale_of(r[r.shape[0] - SCALE_ROWS :, :].astype(jnp.float32)[:1])[0]
        for r in received
    ]


def pieces(rows, body, start):
    def some(i, carry):
        return body(pl.multiple_of(i * STEP, STEP), carry)

    return lax.fori_loop(0, rows // STEP, some, start)


def largest_of(total):
    return jnp.max(jnp.abs(total), axis=0, keepdims=True)


def add_received(source, first, received, rows, sums):
    scales = scales_of([r for r, _ in received])

    def body(at, largest):
        total = source[pl.ds(first + at, STEP), :]
        for (r, begin), scale in zip(received, scales):
            total = total + decode(r[pl.ds(begin + at, STEP), :], scale)
        sums[pl.ds(at, STEP), :] = total
        return jnp.maximum(largest, largest_of(total))

    return pieces(rows, body, jnp.zeros((1, COLS), jnp.float32))


def encode(largest, sums, cols, blocks, out_ref):
    step_code = jnp.ceil(jnp.log2(jnp.maximum(largest, 1e-37)) * 64.0)
    step_code = jnp.clip(step_code, -90.0 * 64.0, 128.0 * 64.0)
    factor = scale_of(step_code)[1]
    rows = len(blocks) * OWN
    out_ref[rows : rows + SCALE_ROWS, :] = (
        jnp.broadcast_to(step_code, (SCALE_ROWS, COLS)).astype(jnp.int32).astype(jnp.int16)
    )
    for slot, block in enumerate(blocks):

        def body(at, _):
            scaled = sums[pl.ds(pl.multiple_of(block * OWN + at, STEP), STEP), cols] * factor
            rooted = scaled * lax.rsqrt(jnp.maximum(jnp.abs(scaled), 1e-12))
            whole = jnp.round(rooted).astype(jnp.int32)
            out_ref[pl.ds(slot * OWN + at, STEP), :] = whole.astype(jnp.int16)
            return 0

        pieces(OWN, body, 0)


def product(x_ref, me_ref, masks, g):
    x = jnp.concatenate([x_ref[0, :, columns_of(me_ref, mask)] for mask in masks], axis=1)
    return lax.dot_general(x, g, TRANSPOSED, preferred_element_type=jnp.float32)


def first_kernel(pair, me_ref, x_ref, g_ref, after_ref, *refs):
    outs, sums = refs[:2], refs[2]
    variants = PAIRS[pair]
    if pair == 0:
        total = lax.dot_general(
            x_ref[:, : 4 * OWN],
            x_ref[:, 4 * OWN :],
            TRANSPOSED,
            preferred_element_type=jnp.float32,
        )
        place = {XA ^ XB ^ y: jnp.bitwise_and(jnp.bitwise_xor(me_ref[0], y), 3) for y in range(4)}
    else:
        masks = masks_of(ORDERS[variants[0]], 0)
        cols = slice(variants[0] * COLS, (variants[1] + 1) * COLS)
        total = product(x_ref, me_ref, masks, g_ref[0, :, cols])
        place = {mask: slot for slot, mask in enumerate(masks)}
    sums[...] = total
    largest = largest_of(total)
    for half, v in enumerate(variants):
        cols = slice(half * COLS, (half + 1) * COLS)
        blocks = [place[mask] for mask in masks_of(ORDERS[v], 0)]
        encode(largest[:, cols], sums, cols, blocks, outs[half])


def mid_kernel(step, has, me_ref, x_ref, g_ref, *refs):
    received = refs[1 : 1 + VARIANTS * has]
    outs = refs[1 + VARIANTS * has :][:VARIANTS]
    sums = refs[-1]
    for v in range(VARIANTS):
        masks = masks_of(ORDERS[v], step)
        total = product(x_ref, me_ref, masks, g_ref[0, :, v * COLS : (v + 1) * COLS])
        into = outs[v] if step == 3 else sums
        into[...] = total
        largest = largest_of(total)
        if has:
            largest = add_received(into, 0, [(received[v], 0)], 4 * OWN, into)
        if step != 3:
            encode(largest, sums, slice(0, COLS), range(4), outs[v])


def late_kernel(count, arrivals, p_ref, *refs):
    received, out, sums = refs[:arrivals], refs[arrivals], refs[arrivals + 1]
    first = count * OWN
    largest = add_received(
        p_ref, first, [(r, first) for r in received], count * OWN, sums
    )
    encode(largest, sums, slice(0, COLS), range(count), out)


def finish_kernel(*refs):
    flag_ref = refs[0]
    grad_hbm, report_hbm, grad_ref, report_ref, sems = refs[-5:]
    copies = []
    acc = jnp.zeros((8, 128), jnp.float32)
    for v in range(VARIANTS):
        p_ref, *received = refs[1 + 4 * v : 5 + 4 * v]
        scales = scales_of(received)

        def body(at, acc):
            total = p_ref[pl.ds(at, STEP), :]
            for r, scale in zip(received, scales):
                total = total + decode(r[pl.ds(at, STEP), :], scale)
            grad_ref[pl.ds(at, STEP), v * COLS : (v + 1) * COLS] = total
            squared = total * total
            squared = squared[:, :128] + squared[:, 128:]
            return acc + jnp.sum(squared.reshape(STEP // 8, 8, 128), axis=0)

        acc = pieces(OWN, body, acc)
        cols = slice(v * COLS, (v + 1) * COLS)
        copies.append(
            pltpu.make_async_copy(grad_ref.at[:, cols], grad_hbm.at[:, cols], sems.at[v])
        )
        copies[-1].start()
    marked = jnp.where(flag_ref[0, 0] != 0, 1.0, 0.0)
    acc = acc + pltpu.roll(acc, 64, axis=1)
    lane = lax.broadcasted_iota(jnp.int32, (8, 128), 1)
    acc = jnp.where(lane < 64, jnp.sum(acc, axis=0, keepdims=True), marked)
    report_ref[...] = jnp.broadcast_to(acc[:1][None], (DEVICES, 1, 128))
    copies.append(pltpu.make_async_copy(report_ref, report_hbm, sems.at[VARIANTS]))
    copies[-1].start()
    for copy in copies:
        copy.wait()


WHOLE = pl.BlockSpec(memory_space=pltpu.VMEM)
LEFT = pl.BlockSpec(memory_space=pl.ANY)
FAR = pl.BlockSpec(memory_space=pltpu.HBM)
SCALAR = pl.BlockSpec(memory_space=pltpu.SMEM)


def coded(blocks):
    return jax.ShapeDtypeStruct((blocks * OWN + SCALE_ROWS, COLS), jnp.int16)


def partial(blocks):
    return jax.ShapeDtypeStruct((blocks * OWN, COLS), jnp.float32)


def cost(blocks, dots, arrivals):
    values = blocks * OWN * COLS
    return pl.CostEstimate(
        flops=2 * TOK * values * dots,
        bytes_accessed=values * (4 + 2 * arrivals),
        transcendentals=values,
    )


def kernel_call(body, name, ins, outs, scratch, estimate, out_spec=WHOLE):
    return pl.pallas_call(
        body,
        out_shape=outs,
        in_specs=ins,
        out_specs=[out_spec] * len(outs),
        scratch_shapes=scratch,
        compiler_params=pltpu.CompilerParams(vmem_limit_bytes=KERNEL_VMEM),
        cost_estimate=estimate,
        name=name,
    )


def first(pair, me, x, g, after):
    return kernel_call(
        functools.partial(first_kernel, pair),
        f"first_{pair}",
        [SCALAR, WHOLE, WHOLE if pair else LEFT, LEFT],
        [coded(4)] * 2,
        [pltpu.VMEM((4 * OWN, 2 * COLS), jnp.float32)],
        cost(8, 1, 1),
    )(me, x, g, after)


def mid(step, me, x, g, after, received):
    return kernel_call(
        functools.partial(mid_kernel, step, 1 if received else 0),
        f"mid_{step}",
        [SCALAR, WHOLE, WHOLE, LEFT] + [WHOLE] * len(received),
        [partial(4) if step == 3 else coded(4)] * VARIANTS,
        [pltpu.VMEM((4 * OWN, COLS), jnp.float32)],
        cost(4 * VARIANTS, 1, 1),
    )(me, x, g, after, *received)


def late(count, v, p, received):
    [code] = kernel_call(
        functools.partial(late_kernel, count, len(received)),
        f"late_{count}_{v}",
        [WHOLE] * (1 + len(received)),
        [coded(count)],
        [pltpu.VMEM((count * OWN, COLS), jnp.float32)],
        cost(count, 0, len(received)),
    )(p, *received)
    return code


def finish(flag, held):
    outs = [
        jax.ShapeDtypeStruct((OWN, KV), jnp.float32),
        jax.ShapeDtypeStruct((DEVICES, 1, 128), jnp.float32),
    ]
    return kernel_call(
        finish_kernel,
        "finish",
        [SCALAR] + [WHOLE] * len(held),
        outs,
        [pltpu.VMEM(o.shape, o.dtype) for o in outs] + [pltpu.SemaphoreType.DMA((VARIANTS + 1,))],
        cost(VARIANTS, 0, 3),
        out_spec=FAR,
    )(flag, *held)


UPDATE_ROWS = 128


def update_kernel(bound, pipe_ref, reports, w_ref, m1_ref, m2_ref, g_ref, *refs):
    new_w, new_m1, new_m2, clip_ref, own_ref = refs

    @pl.when(pl.program_id(0) == 0)
    def _():
        lane = lax.broadcasted_iota(jnp.int32, (1, 128), 1)
        total = jnp.zeros((1, 128), jnp.float32)
        own = jnp.zeros((1, 128), jnp.float32)
        for section in range(PIPE):
            report = functools.reduce(
                jnp.add, [reports[rank * PIPE + section] for rank in range(RANKS)]
            )
            marks = pltpu.roll(report, 64, axis=1)
            total = total + jnp.where((lane < 64) & (marks == 0.0), report, 0.0)
            own = jnp.where(pipe_ref[0] == section, marks, own)
        total = jnp.sum(total, keepdims=True)
        clip = jnp.minimum(1.0, bound / (jnp.sqrt(total) + 1e-06))
        clip_ref[...] = jnp.broadcast_to(clip, (8, 128))
        own_ref[...] = jnp.broadcast_to(own[:1, :1], (8, 128))

    clip = clip_ref[:1, :1]
    keep = own_ref[:1, :1] == 0.0
    w, first_old, second_old = w_ref[0], m1_ref[0], m2_ref[0]
    scaled = clip * g_ref[...]
    first = 0.9 * first_old + 0.1 * scaled
    second = 0.95 * second_old + 0.05 * scaled * scaled
    updated = w - 0.02 * (first / (jnp.sqrt(second) + 1e-08) + 0.1 * w)
    new_w[0] = jnp.where(keep, updated, w)
    new_m1[0] = jnp.where(keep, first, first_old)
    new_m2[0] = jnp.where(keep, second, second_old)


def update(pipe, reports, w, m1, m2, grad, bound):
    block = pl.BlockSpec((1, UPDATE_ROWS, KV), lambda i: (0, i, 0))
    shape = jax.ShapeDtypeStruct((1, OWN, KV), jnp.float32)
    return pl.pallas_call(
        functools.partial(update_kernel, bound),
        grid=(OWN // UPDATE_ROWS,),
        out_shape=[shape] * 3,
        in_specs=[SCALAR, WHOLE, block, block, block]
        + [pl.BlockSpec((UPDATE_ROWS, KV), lambda i: (i, 0))],
        out_specs=[block] * 3,
        scratch_shapes=[pltpu.VMEM((8, 128), jnp.float32)] * 2,
        compiler_params=pltpu.CompilerParams(vmem_limit_bytes=UPDATE_VMEM),
        name="update",
    )(pipe, reports, w, m1, m2, grad)


def swap(value, axis, count, mask):
    return lax.ppermute(value, axis, [(i, i ^ mask) for i in range(count)])


def per_device(layer_input, value_grad, master_weight, moment_one, moment_two, overflow_flags):
    me = lax.axis_index("dp").astype(jnp.int32).reshape(1)
    every = range(VARIANTS)

    def cross(codes, bit):
        return [swap(codes[v], "dp", RANKS, ORDERS[v][bit]) for v in every]

    x, g = layer_input, value_grad
    far = lax.bitwise_xor(lax.axis_index("dp") // 4, 2) * (4 * OWN)
    some = jnp.concatenate(
        [
            lax.dynamic_slice(layer_input[0], (0, far), (TOK, 4 * OWN)),
            value_grad[0, :, PAIRS[0][0] * COLS : (PAIRS[0][1] + 1) * COLS],
        ],
        axis=1,
    )
    codes = first(0, me, some, me, me)
    codes = first(1, me, x, g, codes[-1]) + codes
    zero = cross(codes, 0)
    codes = mid(1, me, x, g, codes[-1], [])
    one = cross(codes, 0)
    codes = mid(2, me, x, g, codes[-1], zero)
    two = cross(codes, 1)
    kept = mid(3, me, x, g, codes[-1], one)
    three = cross([late(2, v, kept[v], [two[v]]) for v in every], 2)
    four = cross([late(1, v, kept[v], [two[v], three[v]]) for v in every], 3)
    held = [a for v in every for a in (kept[v], two[v], three[v], four[v])]
    grad, report = finish(overflow_flags, held)
    reports = lax.all_to_all(report, ("dp", "pipe"), 0, 0)
    bound = 0.5 * math.sqrt(D * KV * PIPE)
    pipe = lax.axis_index("pipe").astype(jnp.int32).reshape(1)
    return tuple(update(pipe, reports, master_weight, moment_one, moment_two, grad, bound))


def solution(mesh):
    placed = P("pipe", "dp", None)
    return jax.shard_map(
        per_device,
        mesh=mesh,
        in_specs=(placed,) * 5 + (P("pipe", "dp"),),
        out_specs=(placed,) * 3,
        check_vma=False,
    )
```

```python
import functools
import math

import jax
import jax.numpy as jnp
from jax import lax
from jax.experimental import pallas as pl
from jax.experimental.pallas import tpu as pltpu
from jax.sharding import PartitionSpec as P

D = 8192
KV = 1024
RANKS = 16
DEVICES = 128
FAR_ROWS = 12288
PIPE = 8
TOK = 512
OWN = 512
COLS = 256
VARIANTS = 4
STEP = 512
KERNEL_VMEM = 14 << 20
HEAD_VMEM = 121 << 19
UPDATE_VMEM = 60 << 20
TOP_POWER = 29.9985
SCALE_ROWS = 16

XA, XB, YA, YB = 4, 12, 1, 3
ORDERS = ((XA, XB, YB, YA), (YA, YB, XB, XA), (YB, YA, XA, XB), (XB, XA, YA, YB))
RAW, CODED = (0, 1), (2, 3)
SHARES = ((0, 128, 0, 1024), (128, 128, 0, 1024), (256, 256, 0, 512), (256, 256, 512, 512))

TRANSPOSED = (((0,), (0,)), ((), ()))


def masks_of(order, step):
    base = {0: order[0] ^ order[1], 1: order[0], 2: order[1], 3: 0}[step]
    return [base, base ^ order[3], base ^ order[2], base ^ order[2] ^ order[3]]


def decode(codes, scale):
    wide = codes.astype(jnp.float32)
    return wide * jnp.abs(wide) * scale


def scale_of(step_code):
    power = step_code * (1.0 / 64.0) - TOP_POWER
    return jnp.exp2(power), jnp.exp2(-power)


def columns_of(me_ref, mask, v):
    block = jnp.bitwise_xor(me_ref[0], mask)
    first, rows = SHARES[v][:2]
    return pl.ds(pl.multiple_of(block * OWN + first, 128), rows)


def scales_of(received):
    return [
        scale_of(r[r.shape[0] - SCALE_ROWS :, :].astype(jnp.float32)[:1])[0]
        for r in received
    ]


def pieces(rows, body, start):
    def some(i, carry):
        return body(pl.multiple_of(i * STEP, STEP), carry)

    return lax.fori_loop(0, rows // STEP, some, start)


def largest_of(total):
    return jnp.max(jnp.abs(total), axis=0, keepdims=True)


def add_received(source, first, received, rows, sums):
    scales = scales_of([r for r, _ in received])

    def body(at, largest):
        total = source[pl.ds(first + at, STEP), :]
        for (r, begin), scale in zip(received, scales):
            total = total + decode(r[pl.ds(begin + at, STEP), :], scale)
        sums[pl.ds(at, STEP), :] = total
        return jnp.maximum(largest, largest_of(total))

    return pieces(rows, body, jnp.zeros((1, COLS), jnp.float32))


def encode(largest, sums, blocks, out_ref):
    step_code = jnp.ceil(jnp.log2(jnp.maximum(largest, 1e-37)) * 64.0)
    step_code = jnp.clip(step_code, -90.0 * 64.0, 128.0 * 64.0)
    factor = scale_of(step_code)[1]
    rows = blocks * OWN
    out_ref[rows : rows + SCALE_ROWS, :] = (
        jnp.broadcast_to(step_code, (SCALE_ROWS, COLS)).astype(jnp.int32).astype(jnp.int16)
    )

    def body(at, _):
        scaled = sums[pl.ds(at, STEP), :] * factor
        rooted = scaled * lax.rsqrt(jnp.maximum(jnp.abs(scaled), 1e-12))
        out_ref[pl.ds(at, STEP), :] = jnp.round(rooted).astype(jnp.int32).astype(jnp.int16)
        return 0

    pieces(rows, body, 0)


def multiply(v, x, g, into):
    _, rows, _, cols = SHARES[v]
    total = lax.dot_general(x, g, TRANSPOSED, preferred_element_type=jnp.float32)
    largest = jnp.zeros((1, COLS), jnp.float32)
    for group in range(cols // COLS):
        part = total[:, group * COLS : (group + 1) * COLS]
        largest = jnp.maximum(largest, largest_of(part))
        for slot in range(4):
            at = slot * OWN + group * rows
            into[at : at + rows, :] = part[slot * rows : (slot + 1) * rows, :]
    return largest


def head_kernel(me_ref, x_hbm, g_hbm, *refs):
    outs, (x_buf, g_buf, sums, sems) = refs[: len(CODED)], refs[len(CODED) :]
    copies = []
    for i, v in enumerate(CODED):
        _, rows, first, cols = SHARES[v]
        at = (slice(None), slice(first, first + cols))
        copies.append(
            [pltpu.make_async_copy(g_hbm.at[0, *at], g_buf.at[*at], sems.at[i, 4])]
            + [
                pltpu.make_async_copy(
                    x_hbm.at[0, :, columns_of(me_ref, mask, v)],
                    x_buf.at[i, :, slot * rows : (slot + 1) * rows],
                    sems.at[i, slot],
                )
                for slot, mask in enumerate(masks_of(ORDERS[v], 0))
            ]
        )
        for copy in copies[-1]:
            copy.start()
    for i, v in enumerate(CODED):
        _, _, first, cols = SHARES[v]
        for copy in copies[i]:
            copy.wait()
        largest = multiply(v, x_buf[i], g_buf[:, first : first + cols], sums)
        encode(largest, sums, 4, outs[i])


def work_kernel(step, variants, unread, me_ref, x_ref, g_ref, *refs):
    refs, arrived = list(refs)[unread:], []
    for v in variants:
        count = 0 if step < 2 else 2 if v in RAW else 1
        arrived.append([refs.pop(0) for _ in range(count)])
    outs, sums = refs[:-1], refs[-1]
    for v, there, out in zip(variants, arrived, outs):
        _, rows, first, cols = SHARES[v]
        x = [x_ref[0, :, columns_of(me_ref, mask, v)] for mask in masks_of(ORDERS[v], step)]
        x, g = jnp.concatenate(x, axis=1), g_ref[0, :, first : first + cols]
        if v in RAW:
            half = slice(4 * rows * (step - 2), 4 * rows * (step - 1))
            x = jnp.concatenate([x, there[1][:, half]], axis=0)
            g = jnp.concatenate([g, there[0][...]], axis=0)
        into = out if step == 3 else sums
        largest = multiply(v, x, g, into)
        if step >= 2 and v in CODED:
            largest = add_received(into, 0, [(there[0], 0)], 4 * OWN, into)
        if step != 3:
            encode(largest, sums, 4, out)


def gather_kernel(me_ref, x_ref, after_ref, *outs):
    for v, out in zip(RAW, outs):
        masks = masks_of(ORDERS[v], 0) + masks_of(ORDERS[v], 1)
        for slot, mask in enumerate(masks):
            out[:, slot * 128 : (slot + 1) * 128] = x_ref[0, :, columns_of(me_ref, mask, v)]


def late_kernel(count, arrivals, p_ref, *refs):
    received, out, sums = refs[:arrivals], refs[arrivals], refs[arrivals + 1]
    first = count * OWN
    largest = add_received(
        p_ref, first, [(r, first) for r in received], count * OWN, sums
    )
    encode(largest, sums, count, out)


def finish_kernel(*refs):
    flag_ref = refs[0]
    grad_hbm, report_hbm, grad_ref, report_ref, sems = refs[-5:]
    copies = []
    acc = jnp.zeros((8, 128), jnp.float32)
    for v in range(VARIANTS):
        p_ref, *received = refs[1 + 4 * v : 5 + 4 * v]
        scales = scales_of(received)
        first, rows, left, cols = SHARES[v]
        for group in range(cols // COLS):
            at = slice(group * rows, (group + 1) * rows)
            total = p_ref[at, :]
            for r, scale in zip(received, scales):
                total = total + decode(r[at, :], scale)
            begin = left + group * COLS
            grad_ref[first : first + rows, begin : begin + COLS] = total
            squared = total * total
            squared = squared[:, :128] + squared[:, 128:]
            acc = acc + jnp.sum(squared.reshape(rows // 8, 8, 128), axis=0)
        at = (slice(first, first + rows), slice(left, left + cols))
        copies.append(pltpu.make_async_copy(grad_ref.at[at], grad_hbm.at[at], sems.at[v]))
        copies[-1].start()
    marked = jnp.where(flag_ref[0, 0] != 0, 1.0, 0.0)
    acc = acc + pltpu.roll(acc, 64, axis=1)
    lane = lax.broadcasted_iota(jnp.int32, (8, 128), 1)
    acc = jnp.where(lane < 64, jnp.sum(acc, axis=0, keepdims=True), marked)
    report_ref[...] = jnp.broadcast_to(acc[:1][None], (DEVICES, 1, 128))
    copies.append(pltpu.make_async_copy(report_ref, report_hbm, sems.at[VARIANTS]))
    copies[-1].start()
    for copy in copies:
        copy.wait()


WHOLE = pl.BlockSpec(memory_space=pltpu.VMEM)
LEFT = pl.BlockSpec(memory_space=pl.ANY)
FAR = pl.BlockSpec(memory_space=pltpu.HBM)
SCALAR = pl.BlockSpec(memory_space=pltpu.SMEM)


def coded(blocks):
    return jax.ShapeDtypeStruct((blocks * OWN + SCALE_ROWS, COLS), jnp.int16)


def partial(blocks):
    return jax.ShapeDtypeStruct((blocks * OWN, COLS), jnp.float32)


def cost(blocks, dots, arrivals):
    values = blocks * OWN * COLS
    return pl.CostEstimate(
        flops=2 * TOK * values * dots,
        bytes_accessed=values * (4 + 2 * arrivals),
        transcendentals=values,
    )


def kernel_call(body, name, ins, outs, scratch, estimate, out_specs=None, vmem=KERNEL_VMEM):
    return pl.pallas_call(
        body,
        out_shape=outs,
        in_specs=ins,
        out_specs=out_specs or [WHOLE] * len(outs),
        scratch_shapes=scratch,
        compiler_params=pltpu.CompilerParams(vmem_limit_bytes=vmem),
        cost_estimate=estimate,
        name=name,
    )


def head(me, x, g):
    rows = SHARES[CODED[0]][1]
    return kernel_call(
        head_kernel,
        "head",
        [SCALAR, FAR, FAR],
        [coded(4)] * len(CODED),
        [
            pltpu.VMEM((len(CODED), TOK, 4 * rows), jnp.bfloat16),
            pltpu.VMEM((TOK, KV), jnp.bfloat16),
            pltpu.VMEM((4 * OWN, COLS), jnp.float32),
            pltpu.SemaphoreType.DMA((len(CODED), 5)),
        ],
        cost(8, 1, 1),
        vmem=HEAD_VMEM,
    )(me, x, g)


def work(step, variants, me, x, g, after, arrived):
    after = after if isinstance(after, list) else [after]
    return kernel_call(
        functools.partial(work_kernel, step, variants, len(after)),
        f"work_{step}_{variants[0]}",
        [SCALAR, WHOLE, WHOLE] + [LEFT] * len(after) + [WHOLE] * len(arrived),
        [partial(4) if step == 3 else coded(4)] * len(variants),
        [pltpu.VMEM((4 * OWN, COLS), jnp.float32)],
        cost(4 * len(variants), 1, 1),
    )(me, x, g, *after, *arrived)


def gather(me, x, after):
    return kernel_call(
        gather_kernel,
        "gather",
        [SCALAR, WHOLE, LEFT],
        [jax.ShapeDtypeStruct((TOK, 8 * 128), jnp.bfloat16)] * 2,
        [],
        cost(4, 0, 1),
    )(me, x, after)


def late(count, v, p, received):
    [code] = kernel_call(
        functools.partial(late_kernel, count, len(received)),
        f"late_{count}_{v}",
        [WHOLE] * (1 + len(received)),
        [coded(count)],
        [pltpu.VMEM((count * OWN, COLS), jnp.float32)],
        cost(count, 0, len(received)),
    )(p, *received)
    return code


def finish(flag, held):
    grad = jax.ShapeDtypeStruct((OWN, KV), jnp.float32)
    report = jax.ShapeDtypeStruct((DEVICES, 1, 128), jnp.float32)
    far = jax.ShapeDtypeStruct((FAR_ROWS, KV), jnp.float32)
    return kernel_call(
        finish_kernel,
        "finish",
        [SCALAR] + [WHOLE] * len(held),
        [far, report],
        [pltpu.VMEM(o.shape, o.dtype) for o in (grad, report)]
        + [pltpu.SemaphoreType.DMA((VARIANTS + 1,))],
        cost(VARIANTS, 0, 3),
        [FAR] * 2,
    )(flag, *held)


UPDATE_ROWS = 128


def update_kernel(bound, pipe_ref, reports, w_ref, m1_ref, m2_ref, g_ref, *refs):
    new_w, new_m1, new_m2, clip_ref, own_ref = refs

    @pl.when(pl.program_id(0) == 0)
    def _():
        lane = lax.broadcasted_iota(jnp.int32, (1, 128), 1)
        total = jnp.zeros((1, 128), jnp.float32)
        own = jnp.zeros((1, 128), jnp.float32)
        for section in range(PIPE):
            report = functools.reduce(
                jnp.add, [reports[rank * PIPE + section] for rank in range(RANKS)]
            )
            marks = pltpu.roll(report, 64, axis=1)
            total = total + jnp.where((lane < 64) & (marks == 0.0), report, 0.0)
            own = jnp.where(pipe_ref[0] == section, marks, own)
        total = jnp.sum(total, keepdims=True)
        clip = jnp.minimum(1.0, bound / (jnp.sqrt(total) + 1e-06))
        clip_ref[...] = jnp.broadcast_to(clip, (8, 128))
        own_ref[...] = jnp.broadcast_to(own[:1, :1], (8, 128))

    clip = clip_ref[:1, :1]
    keep = own_ref[:1, :1] == 0.0
    w, first_old, second_old = w_ref[0], m1_ref[0], m2_ref[0]
    scaled = clip * g_ref[...]
    first = 0.9 * first_old + 0.1 * scaled
    second = 0.95 * second_old + 0.05 * scaled * scaled
    updated = w - 0.02 * (first / (jnp.sqrt(second) + 1e-08) + 0.1 * w)
    new_w[0] = jnp.where(keep, updated, w)
    new_m1[0] = jnp.where(keep, first, first_old)
    new_m2[0] = jnp.where(keep, second, second_old)


def update(pipe, reports, w, m1, m2, grad, bound):
    block = pl.BlockSpec((1, UPDATE_ROWS, KV), lambda i: (0, i, 0))
    shape = jax.ShapeDtypeStruct((1, OWN, KV), jnp.float32)
    return pl.pallas_call(
        functools.partial(update_kernel, bound),
        grid=(OWN // UPDATE_ROWS,),
        out_shape=[shape] * 3,
        in_specs=[SCALAR, WHOLE, block, block, block]
        + [pl.BlockSpec((UPDATE_ROWS, KV), lambda i: (i, 0))],
        out_specs=[block] * 3,
        scratch_shapes=[pltpu.VMEM((8, 128), jnp.float32)] * 2,
        compiler_params=pltpu.CompilerParams(vmem_limit_bytes=UPDATE_VMEM),
        name="update",
    )(pipe, reports, w, m1, m2, grad)


def swap(value, axis, count, mask):
    return lax.ppermute(value, axis, [(i, i ^ mask) for i in range(count)])


def per_device(layer_input, value_grad, master_weight, moment_one, moment_two, overflow_flags):
    me = lax.axis_index("dp").astype(jnp.int32).reshape(1)
    every = range(VARIANTS)

    def cross(value, v, bit):
        return swap(value, "dp", RANKS, ORDERS[v][bit])

    x, g = layer_input, value_grad
    zero, one, two = ([None] * VARIANTS for _ in range(3))
    for v in RAW:
        zero[v] = cross(g[0], v, 0)
    codes = head(me, x, g)
    for v, code in zip(CODED, codes):
        zero[v] = cross(code, v, 0)
    after = codes[-1]
    sent = list(gather(me, x, after))
    after = [sent[-1]] + [zero[v] for v in RAW]
    sent += work(1, CODED, me, x, g, after, [])
    for v in every:
        one[v] = cross(sent[v], v, 0)
    after = sent[-1]
    arrived = {v: [zero[v], one[v]] for v in RAW} | {v: [zero[v]] for v in CODED}
    for variants in (CODED, RAW):
        codes = work(2, variants, me, x, g, after, [a for v in variants for a in arrived[v]])
        for v, code in zip(variants, codes):
            two[v] = cross(code, v, 1)
        after = codes[-1]
    arrived |= {v: [one[v]] for v in CODED}
    kept = work(3, tuple(every), me, x, g, after, [a for v in every for a in arrived[v]])
    three = [cross(late(2, v, kept[v], [two[v]]), v, 2) for v in every]
    four = [cross(late(1, v, kept[v], [two[v], three[v]]), v, 3) for v in every]
    held = [a for v in every for a in (kept[v], two[v], three[v], four[v])]
    grad, report = finish(overflow_flags, held)
    reports = lax.all_to_all(report, ("dp", "pipe"), 0, 0)
    bound = 0.5 * math.sqrt(D * KV * PIPE)
    pipe = lax.axis_index("pipe").astype(jnp.int32).reshape(1)
    return tuple(update(pipe, reports, master_weight, moment_one, moment_two, grad, bound))


def solution(mesh):
    placed = P("pipe", "dp", None)
    return jax.shard_map(
        per_device,
        mesh=mesh,
        in_specs=(placed,) * 5 + (P("pipe", "dp"),),
        out_specs=(placed,) * 3,
        check_vma=False,
    )
```

```python
import functools
import math

import jax
import jax.numpy as jnp
from jax import lax
from jax.experimental import pallas as pl
from jax.experimental.pallas import tpu as pltpu
from jax.sharding import PartitionSpec as P

D = 8192
KV = 1024
RANKS = 16
DEVICES = 128
FAR_ROWS = 12288
PIPE = 8
TOK = 512
OWN = 512
COLS = 256
VARIANTS = 4
STEP = 512
KERNEL_VMEM = 14 << 20
HEAD_VMEM = 57 << 20
UPDATE_VMEM = 60 << 20
TOP_POWER = 29.9985
SCALE_ROWS = 16

XA, XB, YA, YB = 4, 12, 1, 3
ORDERS = (
    ((XA, XB, YB, YA), (YA, YB, XB, XA), (YB, YA, XA, XB), (XB, XA, YA, YB)),
    ((XB, XA, YA, YB), (YB, YA, XA, XB), (YA, YB, XB, XA), (XA, XB, YB, YA)),
)
RAW, CODED = (0, 1), (2, 3)
SHARES = ((0, 128, 0, 1024), (128, 128, 0, 1024), (256, 256, 0, 512), (256, 256, 512, 512))

TRANSPOSED = (((0,), (0,)), ((), ()))


def masks_of(v, step):
    masks = []
    for order in (orders[v] for orders in ORDERS):
        base = {0: order[0] ^ order[1], 1: order[0], 2: order[1], 3: 0}[step]
        masks.append([base, base ^ order[3], base ^ order[2], base ^ order[2] ^ order[3]])
    return list(zip(*masks))


def decode(codes, scale):
    wide = codes.astype(jnp.float32)
    return wide * jnp.abs(wide) * scale


def scale_of(step_code):
    power = step_code * (1.0 / 64.0) - TOP_POWER
    return jnp.exp2(power), jnp.exp2(-power)


def columns_of(me_ref, mask, v):
    block = jnp.bitwise_xor(me_ref[0], jnp.where(me_ref[1] == 0, *mask))
    first, rows = SHARES[v][:2]
    return pl.ds(pl.multiple_of(block * OWN + first, 128), rows)


def scales_of(received):
    return [
        scale_of(r[r.shape[0] - SCALE_ROWS :, :].astype(jnp.float32)[:1])[0]
        for r in received
    ]


def pieces(rows, body, start):
    def some(i, carry):
        return body(pl.multiple_of(i * STEP, STEP), carry)

    return lax.fori_loop(0, rows // STEP, some, start)


def largest_of(total):
    return jnp.max(jnp.abs(total), axis=0, keepdims=True)


def add_received(source, first, received, rows, sums):
    scales = scales_of([r for r, _ in received])

    def body(at, largest):
        total = source[pl.ds(first + at, STEP), :]
        for (r, begin), scale in zip(received, scales):
            total = total + decode(r[pl.ds(begin + at, STEP), :], scale)
        sums[pl.ds(at, STEP), :] = total
        return jnp.maximum(largest, largest_of(total))

    return pieces(rows, body, jnp.zeros((1, COLS), jnp.float32))


def encode(largest, sums, blocks, out_ref):
    step_code = jnp.ceil(jnp.log2(jnp.maximum(largest, 1e-37)) * 64.0)
    step_code = jnp.clip(step_code, -90.0 * 64.0, 128.0 * 64.0)
    factor = scale_of(step_code)[1]
    rows = blocks * OWN
    out_ref[rows : rows + SCALE_ROWS, :] = (
        jnp.broadcast_to(step_code, (SCALE_ROWS, COLS)).astype(jnp.int32).astype(jnp.int16)
    )

    def body(at, _):
        scaled = sums[pl.ds(at, STEP), :] * factor
        rooted = scaled * lax.rsqrt(jnp.maximum(jnp.abs(scaled), 1e-12))
        out_ref[pl.ds(at, STEP), :] = jnp.round(rooted).astype(jnp.int32).astype(jnp.int16)
        return 0

    pieces(rows, body, 0)


def multiply(v, x, g, into):
    _, rows, _, cols = SHARES[v]
    total = lax.dot_general(x, g, TRANSPOSED, preferred_element_type=jnp.float32)
    largest = jnp.zeros((1, COLS), jnp.float32)
    for group in range(cols // COLS):
        part = total[:, group * COLS : (group + 1) * COLS]
        largest = jnp.maximum(largest, largest_of(part))
        for slot in range(4):
            at = slot * OWN + group * rows
            into[at : at + rows, :] = part[slot * rows : (slot + 1) * rows, :]
    return largest


def head_kernel(me_ref, x_hbm, g_hbm, *refs):
    outs, raw, (x_buf, g_buf, sums, sems, raw_sems) = refs[:2], refs[2:4], refs[4:]
    copies, raw_copies = [], []
    for i, v in enumerate(CODED):
        _, rows, first, cols = SHARES[v]
        at = (slice(None), slice(first, first + cols))
        copies.append(
            [pltpu.make_async_copy(g_hbm.at[0, *at], g_buf.at[*at], sems.at[i, 4])]
            + [
                pltpu.make_async_copy(
                    x_hbm.at[0, :, columns_of(me_ref, mask, v)],
                    x_buf.at[i, :, slot * rows : (slot + 1) * rows],
                    sems.at[i, slot],
                )
                for slot, mask in enumerate(masks_of(v, 0))
            ]
        )
        for copy in copies[-1]:
            copy.start()
    for i, v in enumerate(RAW):
        for slot, mask in enumerate(masks_of(v, 0) + masks_of(v, 1)):
            raw_copies.append(
                pltpu.make_async_copy(
                    x_hbm.at[0, :, columns_of(me_ref, mask, v)],
                    raw[i].at[:, slot * 128 : (slot + 1) * 128],
                    raw_sems.at[i, slot],
                )
            )
            raw_copies[-1].start()
    for i, v in enumerate(CODED):
        _, _, first, cols = SHARES[v]
        for copy in copies[i]:
            copy.wait()
        largest = multiply(v, x_buf[i], g_buf[:, first : first + cols], sums)
        encode(largest, sums, 4, outs[i])
    for copy in raw_copies:
        copy.wait()


def work_kernel(step, variants, unread, me_ref, x_ref, g_ref, *refs):
    refs, arrived = list(refs)[unread:], []
    for v in variants:
        count = 0 if step < 2 else 2 if v in RAW else 1
        arrived.append([refs.pop(0) for _ in range(count)])
    outs, sums = refs[:-1], refs[-1]
    for v, there, out in zip(variants, arrived, outs):
        _, rows, first, cols = SHARES[v]
        x = [x_ref[0, :, columns_of(me_ref, mask, v)] for mask in masks_of(v, step)]
        x, g = jnp.concatenate(x, axis=1), g_ref[0, :, first : first + cols]
        if v in RAW:
            half = slice(4 * rows * (step - 2), 4 * rows * (step - 1))
            x = jnp.concatenate([x, there[1][:, half]], axis=0)
            g = jnp.concatenate([g, there[0][...]], axis=0)
        into = out if step == 3 else sums
        largest = multiply(v, x, g, into)
        if step >= 2 and v in CODED:
            largest = add_received(into, 0, [(there[0], 0)], 4 * OWN, into)
        if step != 3:
            encode(largest, sums, 4, out)


def late_kernel(count, arrivals, p_ref, *refs):
    received, out, sums = refs[:arrivals], refs[arrivals], refs[arrivals + 1]
    first = count * OWN
    largest = add_received(
        p_ref, first, [(r, first) for r in received], count * OWN, sums
    )
    encode(largest, sums, count, out)


def sum_kernel(*refs):
    outs = refs[3 * VARIANTS :]
    for v, out in enumerate(outs):
        p_ref, *received = refs[3 * v : 3 * v + 3]
        total = p_ref[:OWN, :]
        for r, scale in zip(received, scales_of(received)):
            total = total + decode(r[:OWN, :], scale)
        out[...] = total


def finish_kernel(*refs):
    flag_ref = refs[0]
    grad_hbm, report_hbm, grad_ref, report_ref, sems = refs[-5:]
    copies = []
    acc = jnp.zeros((8, 128), jnp.float32)
    for v in range(VARIANTS):
        p_ref, *received = refs[1 + 2 * v : 3 + 2 * v]
        scales = scales_of(received)
        first, rows, left, cols = SHARES[v]
        for group in range(cols // COLS):
            at = slice(group * rows, (group + 1) * rows)
            total = p_ref[at, :]
            for r, scale in zip(received, scales):
                total = total + decode(r[at, :], scale)
            begin = left + group * COLS
            grad_ref[first : first + rows, begin : begin + COLS] = total
            squared = total * total
            squared = squared[:, :128] + squared[:, 128:]
            acc = acc + jnp.sum(squared.reshape(rows // 8, 8, 128), axis=0)
        at = (slice(first, first + rows), slice(left, left + cols))
        copies.append(pltpu.make_async_copy(grad_ref.at[at], grad_hbm.at[at], sems.at[v]))
        copies[-1].start()
    marked = jnp.where(flag_ref[0, 0] != 0, 1.0, 0.0)
    acc = acc + pltpu.roll(acc, 64, axis=1)
    lane = lax.broadcasted_iota(jnp.int32, (8, 128), 1)
    acc = jnp.where(lane < 64, jnp.sum(acc, axis=0, keepdims=True), marked)
    report_ref[...] = jnp.broadcast_to(acc[:1][None], (DEVICES, 1, 128))
    copies.append(pltpu.make_async_copy(report_ref, report_hbm, sems.at[VARIANTS]))
    copies[-1].start()
    for copy in copies:
        copy.wait()


WHOLE = pl.BlockSpec(memory_space=pltpu.VMEM)
LEFT = pl.BlockSpec(memory_space=pl.ANY)
FAR = pl.BlockSpec(memory_space=pltpu.HBM)
SCALAR = pl.BlockSpec(memory_space=pltpu.SMEM)


def coded(blocks):
    return jax.ShapeDtypeStruct((blocks * OWN + SCALE_ROWS, COLS), jnp.int16)


def partial(blocks):
    return jax.ShapeDtypeStruct((blocks * OWN, COLS), jnp.float32)


def cost(blocks, dots, arrivals):
    values = blocks * OWN * COLS
    return pl.CostEstimate(
        flops=2 * TOK * values * dots,
        bytes_accessed=values * (4 + 2 * arrivals),
        transcendentals=values,
    )


def kernel_call(body, name, ins, outs, scratch, estimate, out_specs=None, vmem=KERNEL_VMEM):
    return pl.pallas_call(
        body,
        out_shape=outs,
        in_specs=ins,
        out_specs=out_specs or [WHOLE] * len(outs),
        scratch_shapes=scratch,
        compiler_params=pltpu.CompilerParams(vmem_limit_bytes=vmem),
        cost_estimate=estimate,
        name=name,
    )


def head(me, x, g):
    rows = SHARES[CODED[0]][1]
    return kernel_call(
        head_kernel,
        "head",
        [SCALAR, FAR, FAR],
        [coded(4)] * len(CODED) + [jax.ShapeDtypeStruct((TOK, 8 * 128), jnp.bfloat16)] * len(RAW),
        [
            pltpu.VMEM((len(CODED), TOK, 4 * rows), jnp.bfloat16),
            pltpu.VMEM((TOK, KV), jnp.bfloat16),
            pltpu.VMEM((4 * OWN, COLS), jnp.float32),
            pltpu.SemaphoreType.DMA((len(CODED), 5)),
            pltpu.SemaphoreType.DMA((len(RAW), 8)),
        ],
        cost(8, 1, 1),
        vmem=HEAD_VMEM,
    )(me, x, g)


def work(step, variants, me, x, g, after, arrived):
    after = after if isinstance(after, list) else [after]
    return kernel_call(
        functools.partial(work_kernel, step, variants, len(after)),
        f"work_{step}_{variants[0]}",
        [SCALAR, WHOLE, WHOLE] + [LEFT] * len(after) + [WHOLE] * len(arrived),
        [partial(4) if step == 3 else coded(4)] * len(variants),
        [pltpu.VMEM((4 * OWN, COLS), jnp.float32)],
        cost(4 * len(variants), 1, 1),
    )(me, x, g, *after, *arrived)


def late(count, v, p, received):
    [code] = kernel_call(
        functools.partial(late_kernel, count, len(received)),
        f"late_{count}_{v}",
        [WHOLE] * (1 + len(received)),
        [coded(count)],
        [pltpu.VMEM((count * OWN, COLS), jnp.float32)],
        cost(count, 0, len(received)),
    )(p, *received)
    return code


def sum_own(held):
    return kernel_call(
        sum_kernel,
        "sum",
        [WHOLE] * len(held),
        [partial(1)] * VARIANTS,
        [],
        cost(VARIANTS, 0, 2),
    )(*held)


def finish(flag, held):
    grad = jax.ShapeDtypeStruct((OWN, KV), jnp.float32)
    report = jax.ShapeDtypeStruct((DEVICES, 1, 128), jnp.float32)
    far = jax.ShapeDtypeStruct((FAR_ROWS, KV), jnp.float32)
    return kernel_call(
        finish_kernel,
        "finish",
        [SCALAR] + [WHOLE] * len(held),
        [far, report],
        [pltpu.VMEM(o.shape, o.dtype) for o in (grad, report)]
        + [pltpu.SemaphoreType.DMA((VARIANTS + 1,))],
        cost(VARIANTS, 0, 3),
        [FAR] * 2,
    )(flag, *held)


UPDATE_ROWS = 256


def update_kernel(bound, pipe_ref, reports, w_ref, m1_ref, m2_ref, g_ref, *refs):
    new_w, new_m1, new_m2, clip_ref, own_ref = refs

    @pl.when(pl.program_id(0) == 0)
    def _():
        lane = lax.broadcasted_iota(jnp.int32, (1, 128), 1)
        total = jnp.zeros((1, 128), jnp.float32)
        own = jnp.zeros((1, 128), jnp.float32)
        for section in range(PIPE):
            report = functools.reduce(
                jnp.add, [reports[rank * PIPE + section] for rank in range(RANKS)]
            )
            marks = pltpu.roll(report, 64, axis=1)
            total = total + jnp.where((lane < 64) & (marks == 0.0), report, 0.0)
            own = jnp.where(pipe_ref[0] == section, marks, own)
        total = jnp.sum(total, keepdims=True)
        clip = jnp.minimum(1.0, bound / (jnp.sqrt(total) + 1e-06))
        clip_ref[...] = jnp.broadcast_to(clip, (8, 128))
        own_ref[...] = jnp.broadcast_to(own[:1, :1], (8, 128))

    clip = clip_ref[:1, :1]
    keep = own_ref[:1, :1] == 0.0
    w, first_old, second_old = w_ref[0], m1_ref[0], m2_ref[0]
    scaled = clip * g_ref[...]
    first = 0.9 * first_old + 0.1 * scaled
    second = 0.95 * second_old + 0.05 * scaled * scaled
    root = second * lax.rsqrt(second)
    updated = w - 0.02 * (first / (root + 1e-08) + 0.1 * w)
    new_w[0] = jnp.where(keep, updated, w)
    new_m1[0] = jnp.where(keep, first, first_old)
    new_m2[0] = jnp.where(keep, second, second_old)


def update(pipe, reports, w, m1, m2, grad, bound):
    block = pl.BlockSpec((1, UPDATE_ROWS, KV), lambda i: (0, i, 0))
    shape = jax.ShapeDtypeStruct((1, OWN, KV), jnp.float32)
    return pl.pallas_call(
        functools.partial(update_kernel, bound),
        grid=(OWN // UPDATE_ROWS,),
        out_shape=[shape] * 3,
        in_specs=[SCALAR, WHOLE, block, block, block]
        + [pl.BlockSpec((UPDATE_ROWS, KV), lambda i: (i, 0))],
        out_specs=[block] * 3,
        scratch_shapes=[pltpu.VMEM((8, 128), jnp.float32)] * 2,
        compiler_params=pltpu.CompilerParams(vmem_limit_bytes=UPDATE_VMEM),
        name="update",
    )(pipe, reports, w, m1, m2, grad)


def swap(value, masks):
    pairs = []
    for rank in range(RANKS):
        for pipe in range(PIPE):
            pairs.append((rank * PIPE + pipe, (rank ^ masks[pipe % 2]) * PIPE + pipe))
    return lax.ppermute(value, ("dp", "pipe"), pairs)


def per_device(layer_input, value_grad, master_weight, moment_one, moment_two, overflow_flags):
    rank, core = lax.axis_index("dp"), lax.axis_index("pipe") % 2
    me = jnp.stack([rank, core]).astype(jnp.int32)
    every = range(VARIANTS)

    def cross(value, v, bit):
        return swap(value, [orders[v][bit] for orders in ORDERS])

    x, g = layer_input, value_grad
    zero, one, two = ([None] * VARIANTS for _ in range(3))
    for v in RAW:
        zero[v] = cross(g[0], v, 0)
    *codes, raw_0, raw_1 = head(me, x, g)
    for v, code in zip(CODED, codes):
        zero[v] = cross(code, v, 0)
    sent = [raw_0, raw_1, *work(1, CODED, me, x, g, [zero[v] for v in RAW], [])]
    for v in every:
        one[v] = cross(sent[v], v, 0)
    after = sent[-1]
    arrived = {v: [zero[v], one[v]] for v in RAW} | {v: [zero[v]] for v in CODED}
    for variants in (CODED, RAW):
        codes = work(2, variants, me, x, g, after, [a for v in variants for a in arrived[v]])
        for v, code in zip(variants, codes):
            two[v] = cross(code, v, 1)
        after = codes[-1]
    arrived |= {v: [one[v]] for v in CODED}
    kept = work(3, tuple(every), me, x, g, after, [a for v in every for a in arrived[v]])
    three = [cross(late(2, v, kept[v], [two[v]]), v, 2) for v in every]
    four = [cross(late(1, v, kept[v], [two[v], three[v]]), v, 3) for v in every]
    own = sum_own([a for v in every for a in (kept[v], two[v], three[v])])
    held = [a for v in every for a in (own[v], four[v])]
    grad, report = finish(overflow_flags, held)
    reports = lax.all_to_all(report, ("dp", "pipe"), 0, 0)
    bound = 0.5 * math.sqrt(D * KV * PIPE)
    pipe = lax.axis_index("pipe").astype(jnp.int32).reshape(1)
    return tuple(update(pipe, reports, master_weight, moment_one, moment_two, grad, bound))


def solution(mesh):
    placed = P("pipe", "dp", None)
    return jax.shard_map(
        per_device,
        mesh=mesh,
        in_specs=(placed,) * 5 + (P("pipe", "dp"),),
        out_specs=(placed,) * 3,
        check_vma=False,
    )
```

```python
import functools
import math

import jax
import jax.numpy as jnp
from jax import lax
from jax.experimental import pallas as pl
from jax.experimental.pallas import tpu as pltpu
from jax.sharding import PartitionSpec as P

D = 8192
KV = 1024
RANKS = 16
DEVICES = 128
FAR_ROWS = 12288
PIPE = 8
TOK = 512
OWN = 512
COLS = 256
VARIANTS = 2
ROWS = OWN // VARIANTS
BLOCK = ROWS * KV // COLS
GROUPS = KV // COLS
STEP = 512
KERNEL_VMEM = 18 << 20
UPDATE_VMEM = 60 << 20
TOP_POWER = 29.9985
SCALE_ROWS = 16

XA, XB, YA, YB = 4, 12, 1, 3
ORDERS = (
    ((XA, XB, YA, YB), (YA, YB, XA, XB)),
    ((XB, XA, YB, YA), (YB, YA, XB, XA)),
)
EVERY = range(VARIANTS)

TRANSPOSED = (((0,), (0,)), ((), ()))


def masks_of(v, step):
    masks = []
    for order in (orders[v] for orders in ORDERS):
        base = {0: order[0] ^ order[1], 1: order[0], 2: order[1], 3: 0}[step]
        masks.append([base, base ^ order[3], base ^ order[2], base ^ order[2] ^ order[3]])
    return list(zip(*masks))


def decode(codes, scale):
    wide = codes.astype(jnp.float32)
    return wide * jnp.abs(wide) * scale


def scale_of(step_code):
    power = step_code * (1.0 / 64.0) - TOP_POWER
    return jnp.exp2(power), jnp.exp2(-power)


def columns_of(me_ref, mask, v):
    block = jnp.bitwise_xor(me_ref[0], jnp.where(me_ref[1] == 0, *mask))
    return pl.ds(pl.multiple_of(block * OWN + v * ROWS, ROWS), ROWS)


def scales_of(received):
    return [
        scale_of(r[r.shape[0] - SCALE_ROWS :, :].astype(jnp.float32)[:1])[0]
        for r in received
    ]


def pieces(rows, body, start):
    def some(i, carry):
        return body(pl.multiple_of(i * STEP, STEP), carry)

    return lax.fori_loop(0, rows // STEP, some, start)


def largest_of(total):
    return jnp.max(jnp.abs(total), axis=0, keepdims=True)


def add_received(source, first, received, rows, sums):
    scales = scales_of([r for r, _ in received])

    def body(at, largest):
        total = source[pl.ds(first + at, STEP), :]
        for (r, begin), scale in zip(received, scales):
            total = total + decode(r[pl.ds(begin + at, STEP), :], scale)
        sums[pl.ds(at, STEP), :] = total
        return jnp.maximum(largest, largest_of(total))

    return pieces(rows, body, jnp.zeros((1, COLS), jnp.float32))


def encode(largest, sums, rows, out_ref):
    step_code = jnp.ceil(jnp.log2(jnp.maximum(largest, 1e-37)) * 64.0)
    step_code = jnp.clip(step_code, -90.0 * 64.0, 128.0 * 64.0)
    factor = scale_of(step_code)[1]
    out_ref[rows : rows + SCALE_ROWS, :] = (
        jnp.broadcast_to(step_code, (SCALE_ROWS, COLS)).astype(jnp.int32).astype(jnp.int16)
    )

    def body(at, _):
        scaled = sums[pl.ds(at, STEP), :] * factor
        rooted = scaled * lax.rsqrt(jnp.maximum(jnp.abs(scaled), 1e-12))
        out_ref[pl.ds(at, STEP), :] = jnp.round(rooted).astype(jnp.int32).astype(jnp.int16)
        return 0

    pieces(rows, body, 0)


def gather_kernel(me_ref, x_ref, *outs):
    outs = list(outs)
    for step in (0, 1):
        for v in EVERY:
            out = outs.pop(0)
            for slot, mask in enumerate(masks_of(v, step)):
                out[:, slot * ROWS : (slot + 1) * ROWS] = x_ref[0, :, columns_of(me_ref, mask, v)]


def multiply(v, masks, me_ref, x_ref, g_ref, x_there, g_there, into):
    x = [x_ref[0, :, columns_of(me_ref, mask, v)] for mask in masks]
    x = jnp.concatenate([jnp.concatenate(x, axis=1), x_there], axis=0)
    g = jnp.concatenate([g_ref[0], g_there[...]], axis=0)
    total = lax.dot_general(x, g, TRANSPOSED, preferred_element_type=jnp.float32)
    largest = jnp.zeros((1, COLS), jnp.float32)
    for group in range(GROUPS):
        part = total[:, group * COLS : (group + 1) * COLS]
        largest = jnp.maximum(largest, largest_of(part))
        for slot in range(len(masks)):
            at = slot * BLOCK + group * ROWS
            into[at : at + ROWS, :] = part[slot * ROWS : (slot + 1) * ROWS, :]
    return largest


def send_kernel(half, me_ref, x_ref, g_ref, after_ref, *refs):
    g_there, x_there, outs, sums = refs[:2], refs[2:4], refs[4:6], refs[6]
    for v in EVERY:
        masks = masks_of(v, 2)[2 * half : 2 * half + 2]
        x = x_there[v][:, 2 * half * ROWS : 2 * (half + 1) * ROWS]
        largest = multiply(v, masks, me_ref, x_ref, g_ref, x, g_there[v], sums)
        encode(largest, sums, 2 * BLOCK, outs[v])


def keep_kernel(me_ref, x_ref, g_ref, after_ref, *refs):
    g_there, x_there, outs = refs[:2], refs[2:4], refs[4:6]
    for v in EVERY:
        multiply(v, masks_of(v, 3), me_ref, x_ref, g_ref, x_there[v][...], g_there[v], outs[v])


def late_kernel(block, begins, p_ref, *refs):
    received, out, sums = refs[:-2], refs[-2], refs[-1]
    received = [(r, begin * BLOCK) for r, begin in zip(received, begins)]
    largest = add_received(p_ref, block * BLOCK, received, BLOCK, sums)
    encode(largest, sums, BLOCK, out)


def sum_kernel(*refs):
    outs = refs[3 * VARIANTS :]
    for v, out in enumerate(outs):
        p_ref, *received = refs[3 * v : 3 * v + 3]
        add_received(p_ref, 0, [(r, 0) for r in received], BLOCK, out)


def finish_kernel(*refs):
    flag_ref = refs[0]
    grad_hbm, report_hbm, grad_ref, report_ref, sems = refs[-5:]
    copies = []
    acc = jnp.zeros((8, 128), jnp.float32)
    for v in EVERY:
        p_ref, r = refs[1 + 2 * v : 3 + 2 * v]
        [scale] = scales_of([r])
        for group in range(GROUPS):
            at = slice(group * ROWS, (group + 1) * ROWS)
            total = p_ref[at, :] + decode(r[at, :], scale)
            grad_ref[v * ROWS : (v + 1) * ROWS, group * COLS : (group + 1) * COLS] = total
            squared = total * total
            squared = squared[:, :128] + squared[:, 128:]
            acc = acc + jnp.sum(squared.reshape(ROWS // 8, 8, 128), axis=0)
        at = slice(v * ROWS, (v + 1) * ROWS)
        copies.append(pltpu.make_async_copy(grad_ref.at[at], grad_hbm.at[at], sems.at[v]))
        copies[-1].start()
    marked = jnp.where(flag_ref[0, 0] != 0, 1.0, 0.0)
    acc = acc + pltpu.roll(acc, 64, axis=1)
    lane = lax.broadcasted_iota(jnp.int32, (8, 128), 1)
    acc = jnp.where(lane < 64, jnp.sum(acc, axis=0, keepdims=True), marked)
    report_ref[...] = jnp.broadcast_to(acc[:1][None], (DEVICES, 1, 128))
    copies.append(pltpu.make_async_copy(report_ref, report_hbm, sems.at[VARIANTS]))
    copies[-1].start()
    for copy in copies:
        copy.wait()


WHOLE = pl.BlockSpec(memory_space=pltpu.VMEM)
LEFT = pl.BlockSpec(memory_space=pl.ANY)
FAR = pl.BlockSpec(memory_space=pltpu.HBM)
SCALAR = pl.BlockSpec(memory_space=pltpu.SMEM)


def coded(blocks):
    return jax.ShapeDtypeStruct((blocks * BLOCK + SCALE_ROWS, COLS), jnp.int16)


def partial(blocks):
    return jax.ShapeDtypeStruct((blocks * BLOCK, COLS), jnp.float32)


def cost(blocks, dots, arrivals):
    values = blocks * BLOCK * COLS
    return pl.CostEstimate(
        flops=4 * TOK * values * dots,
        bytes_accessed=values * (4 + 2 * arrivals),
        transcendentals=values,
    )


def kernel_call(body, name, ins, outs, scratch, estimate, out_specs=None, vmem=KERNEL_VMEM):
    return pl.pallas_call(
        body,
        out_shape=outs,
        in_specs=ins,
        out_specs=out_specs or [WHOLE] * len(outs),
        scratch_shapes=scratch,
        compiler_params=pltpu.CompilerParams(vmem_limit_bytes=vmem),
        cost_estimate=estimate,
        name=name,
    )


def gather(me, x):
    return kernel_call(
        gather_kernel,
        "gather",
        [SCALAR, WHOLE],
        [jax.ShapeDtypeStruct((TOK, 4 * ROWS), jnp.bfloat16)] * (2 * VARIANTS),
        [],
        cost(4 * VARIANTS, 0, 1),
    )(me, x)


def send(half, me, x, g, after, there):
    return kernel_call(
        functools.partial(send_kernel, half),
        f"send_{half}",
        [SCALAR, WHOLE, WHOLE, LEFT] + [WHOLE] * len(there),
        [coded(2)] * VARIANTS,
        [pltpu.VMEM((2 * BLOCK, COLS), jnp.float32)],
        cost(2 * VARIANTS, 1, 1),
    )(me, x, g, after, *there)


def keep(me, x, g, after, there):
    return kernel_call(
        keep_kernel,
        "keep",
        [SCALAR, WHOLE, WHOLE, LEFT] + [WHOLE] * len(there),
        [partial(4)] * VARIANTS,
        [],
        cost(4 * VARIANTS, 1, 1),
    )(me, x, g, after, *there)


def late(block, v, p, received, begins):
    [code] = kernel_call(
        functools.partial(late_kernel, block, begins),
        f"late_{block}_{v}",
        [WHOLE] * (1 + len(received)),
        [coded(1)],
        [pltpu.VMEM((BLOCK, COLS), jnp.float32)],
        cost(1, 0, len(received)),
    )(p, *received)
    return code


def sum_own(held):
    return kernel_call(
        sum_kernel,
        "sum",
        [WHOLE] * len(held),
        [partial(1)] * VARIANTS,
        [],
        cost(VARIANTS, 0, 2),
    )(*held)


def finish(flag, held):
    grad = jax.ShapeDtypeStruct((OWN, KV), jnp.float32)
    report = jax.ShapeDtypeStruct((DEVICES, 1, 128), jnp.float32)
    far = jax.ShapeDtypeStruct((FAR_ROWS, KV), jnp.float32)
    return kernel_call(
        finish_kernel,
        "finish",
        [SCALAR] + [WHOLE] * len(held),
        [far, report],
        [pltpu.VMEM(o.shape, o.dtype) for o in (grad, report)]
        + [pltpu.SemaphoreType.DMA((VARIANTS + 1,))],
        cost(VARIANTS, 0, 1),
        [FAR] * 2,
    )(flag, *held)


UPDATE_ROWS = 256


def update_kernel(bound, pipe_ref, reports, w_ref, m1_ref, m2_ref, g_ref, *refs):
    new_w, new_m1, new_m2, clip_ref, own_ref = refs

    @pl.when(pl.program_id(0) == 0)
    def _():
        lane = lax.broadcasted_iota(jnp.int32, (1, 128), 1)
        total = jnp.zeros((1, 128), jnp.float32)
        own = jnp.zeros((1, 128), jnp.float32)
        for section in range(PIPE):
            report = functools.reduce(
                jnp.add, [reports[rank * PIPE + section] for rank in range(RANKS)]
            )
            marks = pltpu.roll(report, 64, axis=1)
            total = total + jnp.where((lane < 64) & (marks == 0.0), report, 0.0)
            own = jnp.where(pipe_ref[0] == section, marks, own)
        total = jnp.sum(total, keepdims=True)
        clip = jnp.minimum(1.0, bound / (jnp.sqrt(total) + 1e-06))
        clip_ref[...] = jnp.broadcast_to(clip, (8, 128))
        own_ref[...] = jnp.broadcast_to(own[:1, :1], (8, 128))

    clip = clip_ref[:1, :1]
    keep = own_ref[:1, :1] == 0.0
    w, first_old, second_old = w_ref[0], m1_ref[0], m2_ref[0]
    scaled = clip * g_ref[...]
    first = 0.9 * first_old + 0.1 * scaled
    second = 0.95 * second_old + 0.05 * scaled * scaled
    root = second * lax.rsqrt(second)
    updated = w - 0.02 * (first / (root + 1e-08) + 0.1 * w)
    new_w[0] = jnp.where(keep, updated, w)
    new_m1[0] = jnp.where(keep, first, first_old)
    new_m2[0] = jnp.where(keep, second, second_old)


def update(pipe, reports, w, m1, m2, grad, bound):
    block = pl.BlockSpec((1, UPDATE_ROWS, KV), lambda i: (0, i, 0))
    shape = jax.ShapeDtypeStruct((1, OWN, KV), jnp.float32)
    return pl.pallas_call(
        functools.partial(update_kernel, bound),
        grid=(OWN // UPDATE_ROWS,),
        out_shape=[shape] * 3,
        in_specs=[SCALAR, WHOLE, block, block, block]
        + [pl.BlockSpec((UPDATE_ROWS, KV), lambda i: (i, 0))],
        out_specs=[block] * 3,
        scratch_shapes=[pltpu.VMEM((8, 128), jnp.float32)] * 2,
        compiler_params=pltpu.CompilerParams(vmem_limit_bytes=UPDATE_VMEM),
        name="update",
    )(pipe, reports, w, m1, m2, grad)


def swap(value, masks):
    pairs = []
    for rank in range(RANKS):
        for pipe in range(PIPE):
            pairs.append((rank * PIPE + pipe, (rank ^ masks[pipe % 2]) * PIPE + pipe))
    return lax.ppermute(value, ("dp", "pipe"), pairs)


def per_device(layer_input, value_grad, master_weight, moment_one, moment_two, overflow_flags):
    rank, core = lax.axis_index("dp"), lax.axis_index("pipe") % 2
    me = jnp.stack([rank, core]).astype(jnp.int32)

    def cross(values, bit):
        return [swap(value, [orders[v][bit] for orders in ORDERS]) for v, value in enumerate(values)]

    x, g = layer_input, value_grad
    g_there = cross([g[0]] * VARIANTS, 0)
    sent = gather(me, x)
    on_there, kept_there = cross(sent[:VARIANTS], 0), cross(sent[VARIANTS:], 0)
    urgent = send(1, me, x, g, me, g_there + on_there)
    two_urgent = cross(urgent, 1)
    codes = send(0, me, x, g, urgent[-1], g_there + on_there)
    two = cross(codes, 1)
    kept = keep(me, x, g, codes[-1], g_there + kept_there)
    three_urgent = cross([late(3, v, kept[v], [two_urgent[v]], [1]) for v in EVERY], 2)
    three = cross([late(2, v, kept[v], [two_urgent[v]], [0]) for v in EVERY], 2)
    four = cross([late(1, v, kept[v], [two[v], three_urgent[v]], [1, 0]) for v in EVERY], 3)
    own = sum_own([a for v in EVERY for a in (kept[v], two[v], three[v])])
    held = [a for v in EVERY for a in (own[v], four[v])]
    grad, report = finish(overflow_flags, held)
    reports = lax.all_to_all(report, ("dp", "pipe"), 0, 0)
    bound = 0.5 * math.sqrt(D * KV * PIPE)
    pipe = lax.axis_index("pipe").astype(jnp.int32).reshape(1)
    return tuple(update(pipe, reports, master_weight, moment_one, moment_two, grad, bound))


def solution(mesh):
    placed = P("pipe", "dp", None)
    return jax.shard_map(
        per_device,
        mesh=mesh,
        in_specs=(placed,) * 5 + (P("pipe", "dp"),),
        out_specs=(placed,) * 3,
        check_vma=False,
    )
```

```python
import functools
import math

import jax
import jax.numpy as jnp
from jax import lax
from jax.experimental import pallas as pl
from jax.experimental.pallas import tpu as pltpu
from jax.sharding import PartitionSpec as P

D = 8192
KV = 1024
RANKS = 16
DEVICES = 128
FAR_ROWS = 12288
PIPE = 8
TOK = 512
OWN = 512
COLS = 256
VARIANTS = 2
ROWS = OWN // VARIANTS
BLOCK = ROWS * KV // COLS
GROUPS = KV // COLS
STEP = 512
KERNEL_VMEM = 18 << 20
UPDATE_VMEM = 60 << 20
TOP_POWER = 29.9985
SCALE_ROWS = 16

XA, XB, YA, YB = 4, 12, 1, 3
ORDERS = (
    ((XA, XB, YA, YB), (YA, YB, XA, XB)),
    ((XB, XA, YB, YA), (YB, YA, XB, XA)),
)
EVERY = range(VARIANTS)

TRANSPOSED = (((0,), (0,)), ((), ()))


def masks_of(v, step):
    masks = []
    for order in (orders[v] for orders in ORDERS):
        base = {0: order[0] ^ order[1], 1: order[0], 2: order[1], 3: 0}[step]
        masks.append([base, base ^ order[3], base ^ order[2], base ^ order[2] ^ order[3]])
    return list(zip(*masks))


def decode(codes, scale):
    wide = codes.astype(jnp.float32)
    return wide * jnp.abs(wide) * scale


def scale_of(step_code):
    power = step_code * (1.0 / 64.0) - TOP_POWER
    return jnp.exp2(power), jnp.exp2(-power)


def columns_of(me_ref, mask, v):
    block = jnp.bitwise_xor(me_ref[0], jnp.where(me_ref[1] == 0, *mask))
    return pl.ds(pl.multiple_of(block * OWN + v * ROWS, ROWS), ROWS)


def scales_of(received):
    return [
        scale_of(r[r.shape[0] - SCALE_ROWS :, :].astype(jnp.float32)[:1])[0]
        for r in received
    ]


def pieces(rows, body, start):
    def some(i, carry):
        return body(pl.multiple_of(i * STEP, STEP), carry)

    return lax.fori_loop(0, rows // STEP, some, start)


def largest_of(total):
    return jnp.max(jnp.abs(total), axis=0, keepdims=True)


def add_received(source, first, received, rows, sums):
    scales = scales_of([r for r, _ in received])

    def body(at, largest):
        total = source[pl.ds(first + at, STEP), :]
        for (r, begin), scale in zip(received, scales):
            total = total + decode(r[pl.ds(begin + at, STEP), :], scale)
        sums[pl.ds(at, STEP), :] = total
        return jnp.maximum(largest, largest_of(total))

    return pieces(rows, body, jnp.zeros((1, COLS), jnp.float32))


def encode(largest, sums, rows, out_ref):
    step_code = jnp.ceil(jnp.log2(jnp.maximum(largest, 1e-37)) * 64.0)
    step_code = jnp.clip(step_code, -90.0 * 64.0, 128.0 * 64.0)
    factor = scale_of(step_code)[1]
    out_ref[rows : rows + SCALE_ROWS, :] = (
        jnp.broadcast_to(step_code, (SCALE_ROWS, COLS)).astype(jnp.int32).astype(jnp.int16)
    )

    def body(at, _):
        scaled = sums[pl.ds(at, STEP), :] * factor
        rooted = scaled * lax.rsqrt(jnp.maximum(jnp.abs(scaled), 1e-12))
        out_ref[pl.ds(at, STEP), :] = jnp.round(rooted).astype(jnp.int32).astype(jnp.int16)
        return 0

    pieces(rows, body, 0)


def gather_kernel(me_ref, x_ref, *outs):
    outs = list(outs)
    for step in (0, 1):
        for v in EVERY:
            out = outs.pop(0)
            for slot, mask in enumerate(masks_of(v, step)):
                out[:, slot * ROWS : (slot + 1) * ROWS] = x_ref[0, :, columns_of(me_ref, mask, v)]


def multiply(v, masks, me_ref, x_ref, g_ref, x_there, g_there, into):
    x = [x_ref[0, :, columns_of(me_ref, mask, v)] for mask in masks]
    x = jnp.concatenate([jnp.concatenate(x, axis=1), x_there], axis=0)
    g = jnp.concatenate([g_ref[0], g_there[...]], axis=0)
    total = lax.dot_general(x, g, TRANSPOSED, preferred_element_type=jnp.float32)
    largest = jnp.zeros((1, COLS), jnp.float32)
    for group in range(GROUPS):
        part = total[:, group * COLS : (group + 1) * COLS]
        largest = jnp.maximum(largest, largest_of(part))
        for slot in range(len(masks)):
            at = slot * BLOCK + group * ROWS
            into[at : at + ROWS, :] = part[slot * ROWS : (slot + 1) * ROWS, :]
    return largest


def send_kernel(half, me_ref, x_ref, g_ref, after_ref, *refs):
    g_there, x_there, outs, sums = refs[:2], refs[2:4], refs[4:6], refs[6]
    for v in EVERY:
        masks = masks_of(v, 2)[2 * half : 2 * half + 2]
        x = x_there[v][:, 2 * half * ROWS : 2 * (half + 1) * ROWS]
        largest = multiply(v, masks, me_ref, x_ref, g_ref, x, g_there[v], sums)
        encode(largest, sums, 2 * BLOCK, outs[v])


def keep_kernel(me_ref, x_ref, g_ref, after_ref, *refs):
    g_there, x_there, outs = refs[:2], refs[2:4], refs[4:6]
    for v in EVERY:
        multiply(v, masks_of(v, 3), me_ref, x_ref, g_ref, x_there[v][...], g_there[v], outs[v])


def late_kernel(block, begins, p_ref, *refs):
    received, out, sums = refs[:-2], refs[-2], refs[-1]
    received = [(r, begin * BLOCK) for r, begin in zip(received, begins)]
    largest = add_received(p_ref, block * BLOCK, received, BLOCK, sums)
    encode(largest, sums, BLOCK, out)


def sum_kernel(*refs):
    outs = refs[3 * VARIANTS :]
    for v, out in enumerate(outs):
        p_ref, *received = refs[3 * v : 3 * v + 3]
        add_received(p_ref, 0, [(r, 0) for r in received], BLOCK, out)


def finish_kernel(v, *refs):
    last = v == 0
    grad_hbm, sum_out, grad_ref, sum_ref, sems = refs[-5:]
    p_ref, r = refs[-7:-5]
    acc = refs[0][...] if last else jnp.zeros((8, 128), jnp.float32)
    [scale] = scales_of([r])
    for group in range(GROUPS):
        at = slice(group * ROWS, (group + 1) * ROWS)
        total = p_ref[at, :] + decode(r[at, :], scale)
        grad_ref[:, group * COLS : (group + 1) * COLS] = total
        squared = total * total
        squared = squared[:, :128] + squared[:, 128:]
        acc = acc + jnp.sum(squared.reshape(ROWS // 8, 8, 128), axis=0)
    copies = [pltpu.make_async_copy(grad_ref, grad_hbm.at[pl.ds(v * ROWS, ROWS)], sems.at[0])]
    copies[0].start()
    if last:
        marked = jnp.where(refs[1][0, 0] != 0, 1.0, 0.0)
        acc = acc + pltpu.roll(acc, 64, axis=1)
        lane = lax.broadcasted_iota(jnp.int32, (8, 128), 1)
        acc = jnp.where(lane < 64, jnp.sum(acc, axis=0, keepdims=True), marked)
        sum_ref[...] = jnp.broadcast_to(acc[:1][None], (DEVICES, 1, 128))
        copies.append(pltpu.make_async_copy(sum_ref, sum_out, sems.at[1]))
        copies[1].start()
    else:
        sum_out[...] = acc
    for copy in copies:
        copy.wait()


WHOLE = pl.BlockSpec(memory_space=pltpu.VMEM)
LEFT = pl.BlockSpec(memory_space=pl.ANY)
FAR = pl.BlockSpec(memory_space=pltpu.HBM)
SCALAR = pl.BlockSpec(memory_space=pltpu.SMEM)


def coded(blocks):
    return jax.ShapeDtypeStruct((blocks * BLOCK + SCALE_ROWS, COLS), jnp.int16)


def partial(blocks):
    return jax.ShapeDtypeStruct((blocks * BLOCK, COLS), jnp.float32)


def cost(blocks, dots, arrivals):
    values = blocks * BLOCK * COLS
    return pl.CostEstimate(
        flops=4 * TOK * values * dots,
        bytes_accessed=values * (4 + 2 * arrivals),
        transcendentals=values,
    )


def kernel_call(body, name, ins, outs, scratch, estimate, out_specs=None, vmem=KERNEL_VMEM, aliases=None):
    return pl.pallas_call(
        body,
        out_shape=outs,
        in_specs=ins,
        out_specs=out_specs or [WHOLE] * len(outs),
        input_output_aliases=aliases or {},
        scratch_shapes=scratch,
        compiler_params=pltpu.CompilerParams(vmem_limit_bytes=vmem),
        cost_estimate=estimate,
        name=name,
    )


def gather(me, x):
    return kernel_call(
        gather_kernel,
        "gather",
        [SCALAR, WHOLE],
        [jax.ShapeDtypeStruct((TOK, 4 * ROWS), jnp.bfloat16)] * (2 * VARIANTS),
        [],
        cost(4 * VARIANTS, 0, 1),
    )(me, x)


def send(half, me, x, g, after, there):
    return kernel_call(
        functools.partial(send_kernel, half),
        f"send_{half}",
        [SCALAR, WHOLE, WHOLE, LEFT] + [WHOLE] * len(there),
        [coded(2)] * VARIANTS,
        [pltpu.VMEM((2 * BLOCK, COLS), jnp.float32)],
        cost(2 * VARIANTS, 1, 1),
    )(me, x, g, after, *there)


def keep(me, x, g, after, there):
    return kernel_call(
        keep_kernel,
        "keep",
        [SCALAR, WHOLE, WHOLE, LEFT] + [WHOLE] * len(there),
        [partial(4)] * VARIANTS,
        [],
        cost(4 * VARIANTS, 1, 1),
    )(me, x, g, after, *there)


def late(block, v, p, received, begins):
    [code] = kernel_call(
        functools.partial(late_kernel, block, begins),
        f"late_{block}_{v}",
        [WHOLE] * (1 + len(received)),
        [coded(1)],
        [pltpu.VMEM((BLOCK, COLS), jnp.float32)],
        cost(1, 0, len(received)),
    )(p, *received)
    return code


def sum_own(held):
    return kernel_call(
        sum_kernel,
        "sum",
        [WHOLE] * len(held),
        [partial(1)] * VARIANTS,
        [],
        cost(VARIANTS, 0, 2),
    )(*held)


def finish(v, before, own, code):
    last = v == 0
    far = jax.ShapeDtypeStruct((FAR_ROWS, KV), jnp.float32)
    sums = jax.ShapeDtypeStruct((DEVICES, 1, 128) if last else (8, 128), jnp.float32)
    return kernel_call(
        functools.partial(finish_kernel, v),
        f"finish_{v}",
        [WHOLE, SCALAR, LEFT][: len(before)] + [WHOLE] * 2,
        [far, sums],
        [
            pltpu.VMEM((ROWS, KV), jnp.float32),
            pltpu.VMEM(sums.shape, sums.dtype),
            pltpu.SemaphoreType.DMA((2,)),
        ],
        cost(1, 0, 1),
        [FAR, FAR if last else WHOLE],
        aliases={2: 0} if last else {},
    )(*before, own, code)


UPDATE_ROWS = 128


def update_kernel(bound, pipe_ref, reports, *refs):
    sources, results = refs[:4], refs[4:7]
    buffers, (in_sems, out_sems) = refs[7:11], refs[11:]
    w_ref, m1_ref, m2_ref, g_ref = buffers
    arriving, leaving = [], []
    for part in range(OWN // UPDATE_ROWS):
        at = pl.ds(part * UPDATE_ROWS, UPDATE_ROWS)
        arriving.append([])
        for i, (source, buffer) in enumerate(zip(sources, buffers)):
            source = source.at[0, at] if i < 3 else source.at[at]
            copy = pltpu.make_async_copy(source, buffer.at[at], in_sems.at[part, i])
            copy.start()
            arriving[-1].append(copy)

    lane = lax.broadcasted_iota(jnp.int32, (1, 128), 1)
    total = jnp.zeros((1, 128), jnp.float32)
    own = jnp.zeros((1, 128), jnp.float32)
    for section in range(PIPE):
        report = functools.reduce(
            jnp.add, [reports[rank * PIPE + section] for rank in range(RANKS)]
        )
        marks = pltpu.roll(report, 64, axis=1)
        total = total + jnp.where((lane < 64) & (marks == 0.0), report, 0.0)
        own = jnp.where(pipe_ref[0] == section, marks, own)
    total = jnp.sum(total, keepdims=True)
    clip = jnp.minimum(1.0, bound / (jnp.sqrt(total) + 1e-06))
    keep = own[:1, :1] == 0.0

    for part, copies in enumerate(arriving):
        for copy in copies:
            copy.wait()
        at = slice(part * UPDATE_ROWS, (part + 1) * UPDATE_ROWS)
        w, first_old, second_old = w_ref[at], m1_ref[at], m2_ref[at]
        scaled = clip * g_ref[at]
        first = 0.9 * first_old + 0.1 * scaled
        second = 0.95 * second_old + 0.05 * scaled * scaled
        root = second * lax.rsqrt(second)
        updated = w - 0.02 * (first / (root + 1e-08) + 0.1 * w)
        w_ref[at] = jnp.where(keep, updated, w)
        m1_ref[at] = jnp.where(keep, first, first_old)
        m2_ref[at] = jnp.where(keep, second, second_old)
        for i, (buffer, result) in enumerate(zip(buffers, results)):
            copy = pltpu.make_async_copy(buffer.at[at], result.at[0, at], out_sems.at[part, i])
            copy.start()
            leaving.append(copy)
    for copy in leaving:
        copy.wait()


def update(pipe, reports, w, m1, m2, grad, bound):
    parts = OWN // UPDATE_ROWS
    return kernel_call(
        functools.partial(update_kernel, bound),
        "update",
        [SCALAR, WHOLE] + [FAR] * 4,
        [jax.ShapeDtypeStruct((1, OWN, KV), jnp.float32)] * 3,
        [pltpu.VMEM((OWN, KV), jnp.float32)] * 4
        + [pltpu.SemaphoreType.DMA((parts, 4)), pltpu.SemaphoreType.DMA((parts, 3))],
        cost(4, 0, 1),
        [FAR] * 3,
        UPDATE_VMEM,
    )(pipe, reports, w, m1, m2, grad)


def swap(value, masks):
    pairs = []
    for rank in range(RANKS):
        for pipe in range(PIPE):
            pairs.append((rank * PIPE + pipe, (rank ^ masks[pipe % 2]) * PIPE + pipe))
    return lax.ppermute(value, ("dp", "pipe"), pairs)


def per_device(layer_input, value_grad, master_weight, moment_one, moment_two, overflow_flags):
    rank, core = lax.axis_index("dp"), lax.axis_index("pipe") % 2
    me = jnp.stack([rank, core]).astype(jnp.int32)

    def cross(values, bit):
        return [swap(value, [orders[v][bit] for orders in ORDERS]) for v, value in enumerate(values)]

    x, g = layer_input, value_grad
    g_there = cross([g[0]] * VARIANTS, 0)
    sent = gather(me, x)
    on_there, kept_there = cross(sent[:VARIANTS], 0), cross(sent[VARIANTS:], 0)
    urgent = send(1, me, x, g, me, g_there + on_there)
    two_urgent = cross(urgent, 1)
    codes = send(0, me, x, g, urgent[-1], g_there + on_there)
    two = cross(codes, 1)
    kept = keep(me, x, g, codes[-1], g_there + kept_there)
    three_urgent = cross([late(3, v, kept[v], [two_urgent[v]], [1]) for v in EVERY], 2)
    three = cross([late(2, v, kept[v], [two_urgent[v]], [0]) for v in EVERY], 2)
    four = cross([late(1, v, kept[v], [two[v], three_urgent[v]], [1, 0]) for v in EVERY], 3)
    own = sum_own([a for v in EVERY for a in (kept[v], two[v], three[v])])
    grad, squares = finish(1, [], own[1], four[1])
    grad, report = finish(0, [squares, overflow_flags, grad], own[0], four[0])
    reports = lax.all_to_all(report, ("dp", "pipe"), 0, 0)
    bound = 0.5 * math.sqrt(D * KV * PIPE)
    pipe = lax.axis_index("pipe").astype(jnp.int32).reshape(1)
    return tuple(update(pipe, reports, master_weight, moment_one, moment_two, grad, bound))


def solution(mesh):
    placed = P("pipe", "dp", None)
    return jax.shard_map(
        per_device,
        mesh=mesh,
        in_specs=(placed,) * 5 + (P("pipe", "dp"),),
        out_specs=(placed,) * 3,
        check_vma=False,
    )
```

```python
import functools
import math

import jax
import jax.numpy as jnp
from jax import lax
from jax.experimental import pallas as pl
from jax.experimental.pallas import tpu as pltpu
from jax.sharding import PartitionSpec as P

D = 8192
KV = 1024
RANKS = 16
DEVICES = 128
FAR_ROWS = 12288
PIPE = 8
TOK = 512
OWN = 512
COLS = 256
VARIANTS = 2
ROWS = OWN // VARIANTS
BLOCK = ROWS * KV // COLS
GROUPS = KV // COLS
STEP = 512
KERNEL_VMEM = 18 << 20
UPDATE_VMEM = 60 << 20
TOP_POWER = 29.9985
SCALE_ROWS = 16

XA, XB, YA, YB = 4, 12, 1, 3
ORDERS = (
    ((XA, XB, YB, YA), (YA, YB, XA, XB)),
    ((XB, XA, YA, YB), (YB, YA, XB, XA)),
)
EVERY = range(VARIANTS)

TRANSPOSED = (((0,), (0,)), ((), ()))


def masks_of(v, step):
    masks = []
    for order in (orders[v] for orders in ORDERS):
        base = {0: order[0] ^ order[1], 1: order[0], 2: order[1], 3: 0}[step]
        masks.append([base, base ^ order[3], base ^ order[2], base ^ order[2] ^ order[3]])
    return list(zip(*masks))


def decode(codes, scale):
    wide = codes.astype(jnp.float32)
    return wide * jnp.abs(wide) * scale


def scale_of(step_code):
    power = step_code * (1.0 / 64.0) - TOP_POWER
    return jnp.exp2(power), jnp.exp2(-power)


def columns_of(me_ref, mask, v):
    block = jnp.bitwise_xor(me_ref[0], jnp.where(me_ref[1] == 0, *mask))
    return pl.ds(pl.multiple_of(block * OWN + v * ROWS, ROWS), ROWS)


def scales_of(received):
    return [
        scale_of(r[r.shape[0] - SCALE_ROWS :, :].astype(jnp.float32)[:1])[0]
        for r in received
    ]


def pieces(rows, body, start):
    def some(i, carry):
        return body(pl.multiple_of(i * STEP, STEP), carry)

    return lax.fori_loop(0, rows // STEP, some, start)


def largest_of(total):
    return jnp.max(jnp.abs(total), axis=0, keepdims=True)


def add_received(source, first, received, rows, sums):
    scales = scales_of([r for r, _ in received])

    def body(at, largest):
        total = source[pl.ds(first + at, STEP), :]
        for (r, begin), scale in zip(received, scales):
            total = total + decode(r[pl.ds(begin + at, STEP), :], scale)
        sums[pl.ds(at, STEP), :] = total
        return jnp.maximum(largest, largest_of(total))

    return pieces(rows, body, jnp.zeros((1, COLS), jnp.float32))


def encode(largest, sums, rows, out_ref):
    step_code = jnp.ceil(jnp.log2(jnp.maximum(largest, 1e-37)) * 64.0)
    step_code = jnp.clip(step_code, -90.0 * 64.0, 128.0 * 64.0)
    factor = scale_of(step_code)[1]
    out_ref[rows : rows + SCALE_ROWS, :] = (
        jnp.broadcast_to(step_code, (SCALE_ROWS, COLS)).astype(jnp.int32).astype(jnp.int16)
    )

    def body(at, _):
        scaled = sums[pl.ds(at, STEP), :] * factor
        rooted = scaled * lax.rsqrt(jnp.maximum(jnp.abs(scaled), 1e-12))
        out_ref[pl.ds(at, STEP), :] = jnp.round(rooted).astype(jnp.int32).astype(jnp.int16)
        return 0

    pieces(rows, body, 0)


def gather_kernel(me_ref, x_ref, *outs):
    outs = list(outs)
    for step in (0, 1):
        for v in EVERY:
            out = outs.pop(0)
            for slot, mask in enumerate(masks_of(v, step)):
                out[:, slot * ROWS : (slot + 1) * ROWS] = x_ref[0, :, columns_of(me_ref, mask, v)]


def multiply(v, masks, me_ref, x_ref, g_ref, x_there, g_there, into):
    x = [x_ref[0, :, columns_of(me_ref, mask, v)] for mask in masks]
    x = jnp.concatenate([jnp.concatenate(x, axis=1), x_there], axis=0)
    g = jnp.concatenate([g_ref[0], g_there[...]], axis=0)
    total = lax.dot_general(x, g, TRANSPOSED, preferred_element_type=jnp.float32)
    largest = jnp.zeros((1, COLS), jnp.float32)
    for group in range(GROUPS):
        part = total[:, group * COLS : (group + 1) * COLS]
        largest = jnp.maximum(largest, largest_of(part))
        for slot in range(len(masks)):
            at = slot * BLOCK + group * ROWS
            into[at : at + ROWS, :] = part[slot * ROWS : (slot + 1) * ROWS, :]
    return largest


def send_kernel(half, me_ref, x_ref, g_ref, after_ref, *refs):
    g_there, x_there, outs, sums = refs[:2], refs[2:4], refs[4:6], refs[6]
    for v in EVERY:
        masks = masks_of(v, 2)[2 * half : 2 * half + 2]
        x = x_there[v][:, 2 * half * ROWS : 2 * (half + 1) * ROWS]
        largest = multiply(v, masks, me_ref, x_ref, g_ref, x, g_there[v], sums)
        encode(largest, sums, 2 * BLOCK, outs[v])


def keep_kernel(me_ref, x_ref, g_ref, after_ref, *refs):
    g_there, x_there, outs = refs[:2], refs[2:4], refs[4:6]
    for v in EVERY:
        multiply(v, masks_of(v, 3), me_ref, x_ref, g_ref, x_there[v][...], g_there[v], outs[v])


def late_kernel(block, begins, p_ref, *refs):
    received, out, sums = refs[:-2], refs[-2], refs[-1]
    received = [(r, begin * BLOCK) for r, begin in zip(received, begins)]
    largest = add_received(p_ref, block * BLOCK, received, BLOCK, sums)
    encode(largest, sums, BLOCK, out)


def sum_kernel(*refs):
    outs = refs[3 * VARIANTS :]
    for v, out in enumerate(outs):
        p_ref, *received = refs[3 * v : 3 * v + 3]
        add_received(p_ref, 0, [(r, 0) for r in received], BLOCK, out)


def finish_kernel(v, *refs):
    last = v == 0
    grad_hbm, sum_out, grad_ref, sum_ref, sems = refs[-5:]
    p_ref, r = refs[-7:-5]
    acc = refs[0][...] if last else jnp.zeros((8, 128), jnp.float32)
    [scale] = scales_of([r])
    for group in range(GROUPS):
        at = slice(group * ROWS, (group + 1) * ROWS)
        total = p_ref[at, :] + decode(r[at, :], scale)
        grad_ref[:, group * COLS : (group + 1) * COLS] = total
        squared = total * total
        squared = squared[:, :128] + squared[:, 128:]
        acc = acc + jnp.sum(squared.reshape(ROWS // 8, 8, 128), axis=0)
    copies = [pltpu.make_async_copy(grad_ref, grad_hbm.at[pl.ds(v * ROWS, ROWS)], sems.at[0])]
    copies[0].start()
    if last:
        marked = jnp.where(refs[1][0, 0] != 0, 1.0, 0.0)
        acc = acc + pltpu.roll(acc, 64, axis=1)
        lane = lax.broadcasted_iota(jnp.int32, (8, 128), 1)
        acc = jnp.where(lane < 64, jnp.sum(acc, axis=0, keepdims=True), marked)
        sum_ref[...] = jnp.broadcast_to(acc[:1][None], (DEVICES, 1, 128))
        copies.append(pltpu.make_async_copy(sum_ref, sum_out, sems.at[1]))
        copies[1].start()
    else:
        sum_out[...] = acc
    for copy in copies:
        copy.wait()


WHOLE = pl.BlockSpec(memory_space=pltpu.VMEM)
LEFT = pl.BlockSpec(memory_space=pl.ANY)
FAR = pl.BlockSpec(memory_space=pltpu.HBM)
SCALAR = pl.BlockSpec(memory_space=pltpu.SMEM)


def coded(blocks):
    return jax.ShapeDtypeStruct((blocks * BLOCK + SCALE_ROWS, COLS), jnp.int16)


def partial(blocks):
    return jax.ShapeDtypeStruct((blocks * BLOCK, COLS), jnp.float32)


def cost(blocks, dots, arrivals):
    values = blocks * BLOCK * COLS
    return pl.CostEstimate(
        flops=4 * TOK * values * dots,
        bytes_accessed=values * (4 + 2 * arrivals),
        transcendentals=values,
    )


def kernel_call(body, name, ins, outs, scratch, estimate, out_specs=None, vmem=KERNEL_VMEM, aliases=None):
    return pl.pallas_call(
        body,
        out_shape=outs,
        in_specs=ins,
        out_specs=out_specs or [WHOLE] * len(outs),
        input_output_aliases=aliases or {},
        scratch_shapes=scratch,
        compiler_params=pltpu.CompilerParams(vmem_limit_bytes=vmem),
        cost_estimate=estimate,
        name=name,
    )


def gather(me, x):
    return kernel_call(
        gather_kernel,
        "gather",
        [SCALAR, WHOLE],
        [jax.ShapeDtypeStruct((TOK, 4 * ROWS), jnp.bfloat16)] * (2 * VARIANTS),
        [],
        cost(4 * VARIANTS, 0, 1),
    )(me, x)


def send(half, me, x, g, after, there):
    return kernel_call(
        functools.partial(send_kernel, half),
        f"send_{half}",
        [SCALAR, WHOLE, WHOLE, LEFT] + [WHOLE] * len(there),
        [coded(2)] * VARIANTS,
        [pltpu.VMEM((2 * BLOCK, COLS), jnp.float32)],
        cost(2 * VARIANTS, 1, 1),
    )(me, x, g, after, *there)


def keep(me, x, g, after, there):
    return kernel_call(
        keep_kernel,
        "keep",
        [SCALAR, WHOLE, WHOLE, LEFT] + [WHOLE] * len(there),
        [partial(4)] * VARIANTS,
        [],
        cost(4 * VARIANTS, 1, 1),
    )(me, x, g, after, *there)


def late(block, v, p, received, begins):
    [code] = kernel_call(
        functools.partial(late_kernel, block, begins),
        f"late_{block}_{v}",
        [WHOLE] * (1 + len(received)),
        [coded(1)],
        [pltpu.VMEM((BLOCK, COLS), jnp.float32)],
        cost(1, 0, len(received)),
    )(p, *received)
    return code


def sum_own(held):
    return kernel_call(
        sum_kernel,
        "sum",
        [WHOLE] * len(held),
        [partial(1)] * VARIANTS,
        [],
        cost(VARIANTS, 0, 2),
    )(*held)


def finish(v, before, own, code):
    last = v == 0
    far = jax.ShapeDtypeStruct((FAR_ROWS, KV), jnp.float32)
    sums = jax.ShapeDtypeStruct((DEVICES, 1, 128) if last else (8, 128), jnp.float32)
    return kernel_call(
        functools.partial(finish_kernel, v),
        f"finish_{v}",
        [WHOLE, SCALAR, LEFT][: len(before)] + [WHOLE] * 2,
        [far, sums],
        [
            pltpu.VMEM((ROWS, KV), jnp.float32),
            pltpu.VMEM(sums.shape, sums.dtype),
            pltpu.SemaphoreType.DMA((2,)),
        ],
        cost(1, 0, 1),
        [FAR, FAR if last else WHOLE],
        aliases={2: 0} if last else {},
    )(*before, own, code)


UPDATE_ROWS = 128


def update_kernel(bound, pipe_ref, reports, *refs):
    sources, results = refs[:4], refs[4:7]
    buffers, (in_sems, out_sems) = refs[7:11], refs[11:]
    w_ref, m1_ref, m2_ref, g_ref = buffers
    arriving, leaving = [], []
    for part in range(OWN // UPDATE_ROWS):
        at = pl.ds(part * UPDATE_ROWS, UPDATE_ROWS)
        arriving.append([])
        for i, (source, buffer) in enumerate(zip(sources, buffers)):
            source = source.at[0, at] if i < 3 else source.at[at]
            copy = pltpu.make_async_copy(source, buffer.at[at], in_sems.at[part, i])
            copy.start()
            arriving[-1].append(copy)

    lane = lax.broadcasted_iota(jnp.int32, (1, 128), 1)
    total = jnp.zeros((1, 128), jnp.float32)
    own = jnp.zeros((1, 128), jnp.float32)
    for section in range(PIPE):
        report = functools.reduce(
            jnp.add, [reports[rank * PIPE + section] for rank in range(RANKS)]
        )
        marks = pltpu.roll(report, 64, axis=1)
        total = total + jnp.where((lane < 64) & (marks == 0.0), report, 0.0)
        own = jnp.where(pipe_ref[0] == section, marks, own)
    total = jnp.sum(total, keepdims=True)
    clip = jnp.minimum(1.0, bound / (jnp.sqrt(total) + 1e-06))
    keep = own[:1, :1] == 0.0

    for part, copies in enumerate(arriving):
        for copy in copies:
            copy.wait()
        at = slice(part * UPDATE_ROWS, (part + 1) * UPDATE_ROWS)
        w, first_old, second_old = w_ref[at], m1_ref[at], m2_ref[at]
        scaled = clip * g_ref[at]
        first = 0.9 * first_old + 0.1 * scaled
        second = 0.95 * second_old + 0.05 * scaled * scaled
        root = second * lax.rsqrt(second)
        updated = w - 0.02 * (first / (root + 1e-08) + 0.1 * w)
        w_ref[at] = jnp.where(keep, updated, w)
        m1_ref[at] = jnp.where(keep, first, first_old)
        m2_ref[at] = jnp.where(keep, second, second_old)
        for i, (buffer, result) in enumerate(zip(buffers, results)):
            copy = pltpu.make_async_copy(buffer.at[at], result.at[0, at], out_sems.at[part, i])
            copy.start()
            leaving.append(copy)
    for copy in leaving:
        copy.wait()


def update(pipe, reports, w, m1, m2, grad, bound):
    parts = OWN // UPDATE_ROWS
    return kernel_call(
        functools.partial(update_kernel, bound),
        "update",
        [SCALAR, WHOLE] + [FAR] * 4,
        [jax.ShapeDtypeStruct((1, OWN, KV), jnp.float32)] * 3,
        [pltpu.VMEM((OWN, KV), jnp.float32)] * 4
        + [pltpu.SemaphoreType.DMA((parts, 4)), pltpu.SemaphoreType.DMA((parts, 3))],
        cost(4, 0, 1),
        [FAR] * 3,
        UPDATE_VMEM,
    )(pipe, reports, w, m1, m2, grad)


def swap(value, masks):
    pairs = []
    for rank in range(RANKS):
        for pipe in range(PIPE):
            pairs.append((rank * PIPE + pipe, (rank ^ masks[pipe % 2]) * PIPE + pipe))
    return lax.ppermute(value, ("dp", "pipe"), pairs)


def per_device(layer_input, value_grad, master_weight, moment_one, moment_two, overflow_flags):
    rank, core = lax.axis_index("dp"), lax.axis_index("pipe") % 2
    me = jnp.stack([rank, core]).astype(jnp.int32)

    def cross(values, bit):
        return [swap(value, [orders[v][bit] for orders in ORDERS]) for v, value in enumerate(values)]

    x, g = layer_input, value_grad
    g_there = cross([g[0]] * VARIANTS, 0)
    sent = gather(me, x)
    on_there, kept_there = cross(sent[:VARIANTS], 0), cross(sent[VARIANTS:], 0)
    urgent = send(1, me, x, g, me, g_there + on_there)
    two_urgent = cross(urgent, 1)
    codes = send(0, me, x, g, urgent[-1], g_there + on_there)
    two = cross(codes, 1)
    kept = keep(me, x, g, codes[-1], g_there + kept_there)
    three_urgent = cross([late(3, v, kept[v], [two_urgent[v]], [1]) for v in EVERY], 2)
    three = cross([late(2, v, kept[v], [two_urgent[v]], [0]) for v in EVERY], 2)
    four = cross([late(1, v, kept[v], [two[v], three_urgent[v]], [1, 0]) for v in EVERY], 3)
    own = sum_own([a for v in EVERY for a in (kept[v], two[v], three[v])])
    grad, squares = finish(1, [], own[1], four[1])
    grad, report = finish(0, [squares, overflow_flags, grad], own[0], four[0])
    reports = lax.all_to_all(report, ("dp", "pipe"), 0, 0)
    bound = 0.5 * math.sqrt(D * KV * PIPE)
    pipe = lax.axis_index("pipe").astype(jnp.int32).reshape(1)
    return tuple(update(pipe, reports, master_weight, moment_one, moment_two, grad, bound))


def solution(mesh):
    placed = P("pipe", "dp", None)
    return jax.shard_map(
        per_device,
        mesh=mesh,
        in_specs=(placed,) * 5 + (P("pipe", "dp"),),
        out_specs=(placed,) * 3,
        check_vma=False,
    )
```

```python
import functools
import math

import jax
import jax.numpy as jnp
from jax import lax
from jax.experimental import pallas as pl
from jax.experimental.pallas import tpu as pltpu
from jax.sharding import PartitionSpec as P

D = 8192
KV = 1024
RANKS = 16
DEVICES = 128
FAR_ROWS = 12288
PIPE = 8
TOK = 512
OWN = 512
COLS = 256
VARIANTS = 2
ROWS = OWN // VARIANTS
BLOCK = ROWS * KV // COLS
GROUPS = KV // COLS
STEP = 512
KERNEL_VMEM = 18 << 20
UPDATE_VMEM = 60 << 20
TOP_POWER = 29.9985
SCALE_ROWS = 16

XA, XB, YA, YB = 4, 12, 1, 3
ORDERS = (
    ((XA, XB, YB, YA), (YA, YB, XA, XB)),
    ((XB, XA, YA, YB), (YB, YA, XB, XA)),
)
EVERY = range(VARIANTS)

TRANSPOSED = (((0,), (0,)), ((), ()))


def masks_of(v, step):
    masks = []
    for order in (orders[v] for orders in ORDERS):
        base = {0: order[0] ^ order[1], 1: order[0], 2: order[1], 3: 0}[step]
        masks.append([base, base ^ order[3], base ^ order[2], base ^ order[2] ^ order[3]])
    return list(zip(*masks))


def decode(codes, scale):
    wide = codes.astype(jnp.float32)
    return wide * jnp.abs(wide) * scale


def scale_of(step_code):
    power = step_code * (1.0 / 64.0) - TOP_POWER
    return jnp.exp2(power), jnp.exp2(-power)


def columns_of(me_ref, mask, v):
    block = jnp.bitwise_xor(me_ref[0], jnp.where(me_ref[1] == 0, *mask))
    return pl.ds(pl.multiple_of(block * OWN + v * ROWS, ROWS), ROWS)


def scales_of(received):
    return [
        scale_of(r[r.shape[0] - SCALE_ROWS :, :].astype(jnp.float32)[:1])[0]
        for r in received
    ]


def pieces(rows, body, start):
    def some(i, carry):
        return body(pl.multiple_of(i * STEP, STEP), carry)

    return lax.fori_loop(0, rows // STEP, some, start)


def largest_of(total):
    return jnp.max(jnp.abs(total), axis=0, keepdims=True)


def add_received(source, first, received, rows, sums):
    scales = scales_of([r for r, _ in received])

    def body(at, largest):
        total = source[pl.ds(first + at, STEP), :]
        for (r, begin), scale in zip(received, scales):
            total = total + decode(r[pl.ds(begin + at, STEP), :], scale)
        sums[pl.ds(at, STEP), :] = total
        return jnp.maximum(largest, largest_of(total))

    return pieces(rows, body, jnp.zeros((1, COLS), jnp.float32))


def encode(largest, sums, rows, out_ref):
    step_code = jnp.ceil(jnp.log2(jnp.maximum(largest, 1e-37)) * 64.0)
    step_code = jnp.clip(step_code, -90.0 * 64.0, 128.0 * 64.0)
    factor = scale_of(step_code)[1]
    out_ref[rows : rows + SCALE_ROWS, :] = (
        jnp.broadcast_to(step_code, (SCALE_ROWS, COLS)).astype(jnp.int32).astype(jnp.int16)
    )

    def body(at, _):
        scaled = sums[pl.ds(at, STEP), :] * factor
        rooted = scaled * lax.rsqrt(jnp.maximum(jnp.abs(scaled), 1e-12))
        out_ref[pl.ds(at, STEP), :] = jnp.round(rooted).astype(jnp.int32).astype(jnp.int16)
        return 0

    pieces(rows, body, 0)


def gather_kernel(me_ref, x_ref, *outs):
    outs = list(outs)
    for step in (0, 1):
        for v in EVERY:
            out = outs.pop(0)
            for slot, mask in enumerate(masks_of(v, step)):
                out[:, slot * ROWS : (slot + 1) * ROWS] = x_ref[0, :, columns_of(me_ref, mask, v)]


def multiply(v, masks, me_ref, x_ref, g_ref, x_there, g_there, into):
    x = [x_ref[0, :, columns_of(me_ref, mask, v)] for mask in masks]
    x = jnp.concatenate([jnp.concatenate(x, axis=1), x_there], axis=0)
    g = jnp.concatenate([g_ref[0], g_there[...]], axis=0)
    total = lax.dot_general(x, g, TRANSPOSED, preferred_element_type=jnp.float32)
    largest = jnp.zeros((1, COLS), jnp.float32)
    for group in range(GROUPS):
        part = total[:, group * COLS : (group + 1) * COLS]
        largest = jnp.maximum(largest, largest_of(part))
        for slot in range(len(masks)):
            at = slot * BLOCK + group * ROWS
            into[at : at + ROWS, :] = part[slot * ROWS : (slot + 1) * ROWS, :]
    return largest


def send_kernel(half, me_ref, x_ref, g_ref, after_ref, *refs):
    g_there, x_there, outs, sums = refs[:2], refs[2:4], refs[4:6], refs[6]
    for v in EVERY:
        masks = masks_of(v, 2)[2 * half : 2 * half + 2]
        x = x_there[v][:, 2 * half * ROWS : 2 * (half + 1) * ROWS]
        largest = multiply(v, masks, me_ref, x_ref, g_ref, x, g_there[v], sums)
        encode(largest, sums, 2 * BLOCK, outs[v])


def keep_kernel(me_ref, x_ref, g_ref, after_ref, *refs):
    g_there, x_there, outs = refs[:2], refs[2:4], refs[4:6]
    for v in EVERY:
        multiply(v, masks_of(v, 3), me_ref, x_ref, g_ref, x_there[v][...], g_there[v], outs[v])


def late_kernel(block, begins, p_ref, *refs):
    received, out, sums = refs[:-2], refs[-2], refs[-1]
    received = [(r, begin * BLOCK) for r, begin in zip(received, begins)]
    largest = add_received(p_ref, block * BLOCK, received, BLOCK, sums)
    encode(largest, sums, BLOCK, out)


def sum_kernel(*refs):
    outs = refs[3 * VARIANTS :]
    for v, out in enumerate(outs):
        p_ref, *received = refs[3 * v : 3 * v + 3]
        add_received(p_ref, 0, [(r, 0) for r in received], BLOCK, out)


def finish_kernel(v, *refs):
    last = v == 0
    grad_hbm, sum_out, grad_ref, sum_ref, sems = refs[-5:]
    p_ref, r = refs[-7:-5]
    acc = refs[0][...] if last else jnp.zeros((8, 128), jnp.float32)
    [scale] = scales_of([r])
    copies = []
    for group in range(GROUPS):
        at = slice(group * ROWS, (group + 1) * ROWS)
        total = p_ref[at, :] + decode(r[at, :], scale)
        cols = slice(group * COLS, (group + 1) * COLS)
        grad_ref[:, cols] = total
        there = grad_hbm.at[pl.ds(v * ROWS, ROWS), cols]
        copies.append(pltpu.make_async_copy(grad_ref.at[:, cols], there, sems.at[group]))
        copies[-1].start()
        squared = total * total
        squared = squared[:, :128] + squared[:, 128:]
        acc = acc + jnp.sum(squared.reshape(ROWS // 8, 8, 128), axis=0)
    if last:
        marked = jnp.where(refs[1][0, 0] != 0, 1.0, 0.0)
        acc = acc + pltpu.roll(acc, 64, axis=1)
        lane = lax.broadcasted_iota(jnp.int32, (8, 128), 1)
        acc = jnp.where(lane < 64, jnp.sum(acc, axis=0, keepdims=True), marked)
        sum_ref[...] = jnp.broadcast_to(acc[:1][None], (DEVICES, 1, 128))
        copies.append(pltpu.make_async_copy(sum_ref, sum_out, sems.at[GROUPS]))
        copies[-1].start()
    else:
        sum_out[...] = acc
    for copy in copies:
        copy.wait()


WHOLE = pl.BlockSpec(memory_space=pltpu.VMEM)
LEFT = pl.BlockSpec(memory_space=pl.ANY)
FAR = pl.BlockSpec(memory_space=pltpu.HBM)
SCALAR = pl.BlockSpec(memory_space=pltpu.SMEM)


def coded(blocks):
    return jax.ShapeDtypeStruct((blocks * BLOCK + SCALE_ROWS, COLS), jnp.int16)


def partial(blocks):
    return jax.ShapeDtypeStruct((blocks * BLOCK, COLS), jnp.float32)


def cost(blocks, dots, arrivals):
    values = blocks * BLOCK * COLS
    return pl.CostEstimate(
        flops=4 * TOK * values * dots,
        bytes_accessed=values * (4 + 2 * arrivals),
        transcendentals=values,
    )


def kernel_call(body, name, ins, outs, scratch, estimate, out_specs=None, vmem=KERNEL_VMEM, aliases=None):
    return pl.pallas_call(
        body,
        out_shape=outs,
        in_specs=ins,
        out_specs=out_specs or [WHOLE] * len(outs),
        input_output_aliases=aliases or {},
        scratch_shapes=scratch,
        compiler_params=pltpu.CompilerParams(vmem_limit_bytes=vmem),
        cost_estimate=estimate,
        name=name,
    )


def gather(me, x):
    return kernel_call(
        gather_kernel,
        "gather",
        [SCALAR, WHOLE],
        [jax.ShapeDtypeStruct((TOK, 4 * ROWS), jnp.bfloat16)] * (2 * VARIANTS),
        [],
        cost(4 * VARIANTS, 0, 1),
    )(me, x)


def send(half, me, x, g, after, there):
    return kernel_call(
        functools.partial(send_kernel, half),
        f"send_{half}",
        [SCALAR, WHOLE, WHOLE, LEFT] + [WHOLE] * len(there),
        [coded(2)] * VARIANTS,
        [pltpu.VMEM((2 * BLOCK, COLS), jnp.float32)],
        cost(2 * VARIANTS, 1, 1),
    )(me, x, g, after, *there)


def keep(me, x, g, after, there):
    return kernel_call(
        keep_kernel,
        "keep",
        [SCALAR, WHOLE, WHOLE, LEFT] + [WHOLE] * len(there),
        [partial(4)] * VARIANTS,
        [],
        cost(4 * VARIANTS, 1, 1),
    )(me, x, g, after, *there)


def late(block, v, p, received, begins):
    [code] = kernel_call(
        functools.partial(late_kernel, block, begins),
        f"late_{block}_{v}",
        [WHOLE] * (1 + len(received)),
        [coded(1)],
        [pltpu.VMEM((BLOCK, COLS), jnp.float32)],
        cost(1, 0, len(received)),
    )(p, *received)
    return code


def sum_own(held):
    return kernel_call(
        sum_kernel,
        "sum",
        [WHOLE] * len(held),
        [partial(1)] * VARIANTS,
        [],
        cost(VARIANTS, 0, 2),
    )(*held)


def finish(v, before, own, code):
    last = v == 0
    far = jax.ShapeDtypeStruct((FAR_ROWS, KV), jnp.float32)
    sums = jax.ShapeDtypeStruct((DEVICES, 1, 128) if last else (8, 128), jnp.float32)
    return kernel_call(
        functools.partial(finish_kernel, v),
        f"finish_{v}",
        [WHOLE, SCALAR, LEFT][: len(before)] + [WHOLE] * 2,
        [far, sums],
        [
            pltpu.VMEM((ROWS, KV), jnp.float32),
            pltpu.VMEM(sums.shape, sums.dtype),
            pltpu.SemaphoreType.DMA((GROUPS + 1,)),
        ],
        cost(1, 0, 1),
        [FAR, FAR if last else WHOLE],
        aliases={2: 0} if last else {},
    )(*before, own, code)


UPDATE_ROWS = 128


def update_kernel(bound, pipe_ref, reports, *refs):
    sources, results = refs[:4], refs[4:7]
    buffers, (in_sems, out_sems) = refs[7:11], refs[11:]
    w_ref, m1_ref, m2_ref, g_ref = buffers
    arriving, leaving = [], []
    for part in range(OWN // UPDATE_ROWS):
        at = pl.ds(part * UPDATE_ROWS, UPDATE_ROWS)
        arriving.append([])
        for i, (source, buffer) in enumerate(zip(sources, buffers)):
            source = source.at[0, at] if i < 3 else source.at[at]
            copy = pltpu.make_async_copy(source, buffer.at[at], in_sems.at[part, i])
            copy.start()
            arriving[-1].append(copy)

    lane = lax.broadcasted_iota(jnp.int32, (1, 128), 1)
    total = jnp.zeros((1, 128), jnp.float32)
    own = jnp.zeros((1, 128), jnp.float32)
    for section in range(PIPE):
        report = functools.reduce(
            jnp.add, [reports[rank * PIPE + section] for rank in range(RANKS)]
        )
        marks = pltpu.roll(report, 64, axis=1)
        total = total + jnp.where((lane < 64) & (marks == 0.0), report, 0.0)
        own = jnp.where(pipe_ref[0] == section, marks, own)
    total = jnp.sum(total, keepdims=True)
    clip = jnp.minimum(1.0, bound / (jnp.sqrt(total) + 1e-06))
    keep = own[:1, :1] == 0.0

    for part, copies in enumerate(arriving):
        for copy in copies:
            copy.wait()
        at = slice(part * UPDATE_ROWS, (part + 1) * UPDATE_ROWS)
        w, first_old, second_old = w_ref[at], m1_ref[at], m2_ref[at]
        scaled = clip * g_ref[at]
        first = 0.9 * first_old + 0.1 * scaled
        second = 0.95 * second_old + 0.05 * scaled * scaled
        root = second * lax.rsqrt(second)
        updated = w - 0.02 * (first / (root + 1e-08) + 0.1 * w)
        w_ref[at] = jnp.where(keep, updated, w)
        m1_ref[at] = jnp.where(keep, first, first_old)
        m2_ref[at] = jnp.where(keep, second, second_old)
        for i, (buffer, result) in enumerate(zip(buffers, results)):
            copy = pltpu.make_async_copy(buffer.at[at], result.at[0, at], out_sems.at[part, i])
            copy.start()
            leaving.append(copy)
    for copy in leaving:
        copy.wait()


def update(pipe, reports, w, m1, m2, grad, bound):
    parts = OWN // UPDATE_ROWS
    return kernel_call(
        functools.partial(update_kernel, bound),
        "update",
        [SCALAR, WHOLE] + [FAR] * 4,
        [jax.ShapeDtypeStruct((1, OWN, KV), jnp.float32)] * 3,
        [pltpu.VMEM((OWN, KV), jnp.float32)] * 4
        + [pltpu.SemaphoreType.DMA((parts, 4)), pltpu.SemaphoreType.DMA((parts, 3))],
        cost(4, 0, 1),
        [FAR] * 3,
        UPDATE_VMEM,
    )(pipe, reports, w, m1, m2, grad)


def swap(value, masks):
    pairs = []
    for rank in range(RANKS):
        for pipe in range(PIPE):
            pairs.append((rank * PIPE + pipe, (rank ^ masks[pipe % 2]) * PIPE + pipe))
    return lax.ppermute(value, ("dp", "pipe"), pairs)


def per_device(layer_input, value_grad, master_weight, moment_one, moment_two, overflow_flags):
    rank, core = lax.axis_index("dp"), lax.axis_index("pipe") % 2
    me = jnp.stack([rank, core]).astype(jnp.int32)

    def cross(values, bit):
        return [swap(value, [orders[v][bit] for orders in ORDERS]) for v, value in enumerate(values)]

    x, g = layer_input, value_grad
    g_there = cross([g[0]] * VARIANTS, 0)
    sent = gather(me, x)
    on_there, kept_there = cross(sent[:VARIANTS], 0), cross(sent[VARIANTS:], 0)
    urgent = send(1, me, x, g, me, g_there + on_there)
    two_urgent = cross(urgent, 1)
    codes = send(0, me, x, g, urgent[-1], g_there + on_there)
    two = cross(codes, 1)
    kept = keep(me, x, g, codes[-1], g_there + kept_there)
    three_urgent = cross([late(3, v, kept[v], [two_urgent[v]], [1]) for v in EVERY], 2)
    three = cross([late(2, v, kept[v], [two_urgent[v]], [0]) for v in EVERY], 2)
    four = cross([late(1, v, kept[v], [two[v], three_urgent[v]], [1, 0]) for v in EVERY], 3)
    own = sum_own([a for v in EVERY for a in (kept[v], two[v], three[v])])
    grad, squares = finish(1, [], own[1], four[1])
    grad, report = finish(0, [squares, overflow_flags, grad], own[0], four[0])
    reports = lax.all_to_all(report, ("dp", "pipe"), 0, 0)
    bound = 0.5 * math.sqrt(D * KV * PIPE)
    pipe = lax.axis_index("pipe").astype(jnp.int32).reshape(1)
    return tuple(update(pipe, reports, master_weight, moment_one, moment_two, grad, bound))


def solution(mesh):
    placed = P("pipe", "dp", None)
    return jax.shard_map(
        per_device,
        mesh=mesh,
        in_specs=(placed,) * 5 + (P("pipe", "dp"),),
        out_specs=(placed,) * 3,
        check_vma=False,
    )
```
